32 devices in a mesh: expert: 8 (over z, x), dp: 4 (over y, core).
Axes of the slice: x: 2, y: 2, z: 4, core: 2. Of those that a mesh axis runs over, the one named last changes fastest.
Arguments:
- tokens: bfloat16 [1024, 3584], P('expert', 'dp'), may hold values from -6 to 6
- routes: int32 [1024, 2], P('expert'), may hold values from 0 to 3, all different within a row; in each aligned block of 128 rows (0 to 127, 128 to 255, ...) at most 96 rows name the same one
- logits: float32 [1024, 2], P('expert'), may hold values from -6 to 6
- cotangent: bfloat16 [1024, 3584], P('expert', 'dp'), may hold values from -6 to 6
- pair_flags: int32 [2], replicated, may hold values from -1000 to 999
- w_up: bfloat16 [3584, 4096], P('dp', 'expert'), may hold values from -0.09375 to 0.09375
- w_down: bfloat16 [3584, 4096], P('dp', 'expert'), may hold values from -0.1875 to 0.1875
Outputs:
- grad_tokens: bfloat16 [1024, 3584], P('expert', 'dp')
- grad_logits: float32 [1024, 2], P('expert')
- grad_up: bfloat16 [3584, 4096], P('dp', 'expert')
- grad_down: bfloat16 [3584, 4096], P('dp', 'expert')
The draws below stay inside these ranges and needn't reach their ends.
Inputs may be any that keep to these rules, and one draw needn't show every extreme that they name: `routes`: among the 128 tokens of one index of the expert axis no expert is named more than 96 times, a bound that some block reaches; a token names 2 distinct experts.
All inputs are finite; a program needn't handle non-finite values.
Results may differ from the reference program's by a relative error of at most 0.02.
Values may be sent and summed in bfloat16 or wider, within the bound.
A program may use at most 64 MiB of HBM per device.

```python
import math
import jax
import jax.numpy as jnp
import numpy as np
from jax import lax

D = 3584
FF = 1024
TOPK = 2
TOK_DEV = 128
EXPERTS = 4
HALF = 2
CAP = 96
TOKENS = 1024
N_EXPERT = 8


def block_levels(key, shape, cuts, smallest, high):
    def one(position, shards_of):
        draws = jax.random.uniform(jax.random.fold_in(jax.random.fold_in(key, 6), position), (shards_of,), jnp.float32, smallest / len(cuts), high / len(cuts))
        return jnp.repeat(jnp.exp(draws), shape[position] // shards_of).reshape((-1,) + (1,) * (len(shape) - position - 1))

    gain = one(*cuts[0])
    for cut in cuts[1:]:
        gain = gain * one(*cut)
    return gain


def assign_block(own_key, own, number, rows, amount, top, reach, skew):
    sequence = jax.random.permutation(own_key, amount)
    packed, usual = portions_of(amount, rows * top, reach, skew, True), portions_of(amount, rows * top, reach, skew, False)
    places = jnp.arange(amount)

    def named(tallies, rotation):
        used = int((tallies > 0).sum())
        fixed = max(1, used // 4)
        shifted = fixed + (places - fixed + rotation * (used - fixed)) % max(1, amount - fixed)
        return jnp.zeros((amount,), jnp.int32).at[sequence[jnp.where(places < fixed, places, shifted)]].set(jnp.asarray(tallies, jnp.int32))

    tallies = jnp.where(number % 4 == 0, named(packed, number // 4), named(usual, number - number // 4 - 1))
    mixed = jax.random.permutation(jax.random.fold_in(own, 3), amount)
    donor, sink = mixed[0:amount // 2 * 2:2], mixed[1:amount // 2 * 2:2]
    slack = jnp.minimum(tallies[donor] - 1, reach - tallies[sink]) // 2
    slack = jnp.where((donor == sequence[0]) | (sink == sequence[0]) | (tallies[sink] == 0), 0, jnp.maximum(slack, 0))
    shifted = jax.random.randint(jax.random.fold_in(own, 4), (amount // 2,), 0, 1 << 20) % (slack + 1)
    tallies = tallies.at[donor].add(-shifted).at[sink].add(shifted)
    members = jnp.searchsorted(jnp.cumsum(tallies), jnp.arange(rows * top), side="right").astype(jnp.int32)
    listing = members.reshape(top, rows).T
    listing = listing[jax.random.permutation(jax.random.fold_in(own, 1), rows)]
    rotation = jax.random.randint(jax.random.fold_in(own, 2), (rows, 1), 0, top)
    return jnp.take_along_axis(listing, (jnp.arange(top)[None, :] + rotation) % top, axis=1)


def portions_of(count, total, reach, skew, full):
    weights = [(1 << 20) // math.isqrt(grade ** skew) + 1 for grade in range(1, count + 1)]
    largest = reach if full else min(reach, max(-(-total // count), total * weights[0] // sum(weights)))
    least = 1 if total - largest >= count - 1 else 0
    given, rest = [largest] + [least] * (count - 1), total - largest - least * (count - 1)
    while rest > 0:
        candidates = [i for i in range(1, count) if given[i] < largest] or [i for i in range(1, count) if given[i] < reach]
        mass, left = sum([weights[i] for i in candidates]), rest
        for i in candidates:
            more = min(reach - given[i], max(1, left * weights[i] // mass), rest)
            given[i] = given[i] + more
            rest = rest - more
    return np.array(given)


def centred(key, dims, width, most, cuts=(), held_as=jnp.bfloat16):
    gain = block_levels(key, dims, cuts, -0.22, 0.18) if cuts else 1.0
    drawn = jax.random.normal(key, dims, jnp.float32) * width * gain
    return jnp.minimum(jnp.maximum(drawn, -most), most).astype(held_as)


def setup_inputs(seed: int = 0) -> dict:
    splits = jax.random.split(jax.random.key(seed), 8)
    tokens = centred(splits[0], (TOKENS, D), 1.0, 6.0, ((0, 8), (1, 4)))
    routes_keys = jax.random.split(jax.random.fold_in(splits[1], 1), TOKENS // TOK_DEV)
    routes_turns = jax.random.permutation(jax.random.fold_in(splits[1], 3), TOKENS // TOK_DEV)
    routes = jax.vmap(lambda own, number: assign_block(jax.random.fold_in(splits[1], 2), own, number, TOK_DEV, EXPERTS, TOPK, CAP, 2))(routes_keys, routes_turns).reshape((TOKENS, TOPK))
    logits = centred(splits[2], (TOKENS, TOPK), 2.0, 6.0, ((0, 8),), jnp.float32)
    cotangent = centred(splits[3], (TOKENS, D), 1.0, 6.0, ((0, 8), (1, 4)))
    pair_flags = jax.random.randint(splits[4], (HALF,), -1000, 1000).astype(jnp.int32)
    w_up = centred(splits[5], (D, EXPERTS * FF), D ** -0.5, 0.09375, ((0, 4), (1, 8)))
    w_down = centred(splits[6], (D, EXPERTS * FF), FF ** -0.5, 0.1875, ((0, 4), (1, 8)))
    return dict(tokens=tokens, routes=routes, logits=logits, cotangent=cotangent, pair_flags=pair_flags, w_up=w_up, w_down=w_down)


def reference(tokens, routes, logits, cotangent, pair_flags, w_up, w_down):
    per_block = TOK_DEV * TOPK
    route_total = N_EXPERT * per_block
    half_width = FF // 2
    expert_ids = jnp.arange(EXPERTS, dtype=jnp.int32)
    paired = jnp.concatenate([pair_flags, pair_flags]) > 0
    owner_slot = jnp.where(paired, (expert_ids + HALF) % EXPERTS, expert_ids).astype(jnp.int32)
    affinity = jax.nn.sigmoid(logits)
    weights = affinity / jnp.sum(affinity, -1, keepdims=True)
    flat_weights = weights.reshape(-1)
    grouped = routes.reshape(N_EXPERT, per_block).astype(jnp.int32)
    onehot = (grouped[:, :, None] == expert_ids[None, None, :]).astype(jnp.int32)
    slot_rank = (jnp.sum(jnp.cumsum(onehot, 1) * onehot, -1) - 1).astype(jnp.int32)
    block_ids = jnp.broadcast_to(jnp.arange(N_EXPERT, dtype=jnp.int32)[:, None], (N_EXPERT, per_block))
    route_ids = jnp.arange(route_total, dtype=jnp.int32).reshape(N_EXPERT, per_block)
    slot_table = jnp.full((EXPERTS, N_EXPERT, CAP), route_total, jnp.int32).at[grouped, block_ids, slot_rank].set(route_ids)
    up_blocks = w_up.reshape(D, EXPERTS, FF).transpose(1, 0, 2)
    down_blocks = w_down.reshape(D, EXPERTS, FF).transpose(1, 0, 2)

    def one_expert(totals, expert_item):
        grad_acc, pair_acc = totals
        slot_rows, up_block, down_block = expert_item
        row_index = slot_rows.reshape(-1)
        filled = row_index < route_total
        safe_index = jnp.where(filled, row_index, 0)
        token_index = safe_index // TOPK
        x_rows = jnp.where(filled[:, None], tokens[token_index], jnp.zeros((), tokens.dtype))
        c_rows = (flat_weights[safe_index][:, None] * cotangent[token_index].astype(jnp.float32)).astype(jnp.bfloat16)
        c_rows = jnp.where(filled[:, None], c_rows, jnp.zeros((), jnp.bfloat16))
        up_pre = jnp.dot(x_rows, up_block, preferred_element_type=jnp.float32)
        up_sig = jax.nn.sigmoid(up_pre)
        hidden = (up_pre * up_sig).astype(jnp.bfloat16)
        grad_hidden = jnp.dot(c_rows, down_block, preferred_element_type=jnp.float32)
        pair_halves = jnp.sum((hidden.astype(jnp.float32) * grad_hidden).reshape(-1, 2, half_width), -1).astype(jnp.bfloat16)
        grad_pre = (grad_hidden * up_sig * (1.0 + up_pre * (1.0 - up_sig))).astype(jnp.bfloat16)
        route_halves = jnp.einsum('nhf,dhf->nhd', grad_pre.astype(jnp.float32).reshape(-1, 2, half_width), up_block.astype(jnp.float32).reshape(D, 2, half_width)).astype(jnp.bfloat16)
        route_sum = jnp.sum(route_halves.astype(jnp.float32), 1)
        grad_up_e = jnp.dot(x_rows.T, grad_pre, preferred_element_type=jnp.float32).astype(jnp.bfloat16)
        grad_down_e = jnp.dot(c_rows.T, hidden, preferred_element_type=jnp.float32).astype(jnp.bfloat16)
        token_target = jnp.where(filled, token_index, TOKENS)
        grad_acc = grad_acc.at[token_target].add(route_sum, mode="drop")
        pair_target = jnp.where(filled, row_index, route_total)
        pair_acc = pair_acc.at[pair_target].set(jnp.sum(pair_halves.astype(jnp.float32), 1), mode="drop")
        return (grad_acc, pair_acc), (grad_up_e, grad_down_e)

    start = (jnp.zeros((TOKENS, D), jnp.float32), jnp.zeros((route_total,), jnp.float32))
    (grad_acc, pair_acc), (up_all, down_all) = lax.scan(one_expert, start, (slot_table, up_blocks, down_blocks))
    grad_tokens = grad_acc.astype(jnp.bfloat16)
    pairing_all = pair_acc.reshape(TOKENS, TOPK)
    grad_logits = (1.0 - affinity) * (pairing_all - weights * jnp.sum(pairing_all, -1, keepdims=True))
    grad_up = up_all[owner_slot].transpose(1, 0, 2).reshape(D, EXPERTS * FF)
    grad_down = down_all[owner_slot].transpose(1, 0, 2).reshape(D, EXPERTS * FF)
    return grad_tokens, grad_logits, grad_up, grad_down
```

```python
import jax
import jax.numpy as jnp
from jax import lax
from jax.sharding import PartitionSpec as P


def passed_along(value, axis, steps):
    count = lax.axis_size(axis)
    pairs = [(source, (source + steps) % count) for source in range(count)]
    return lax.ppermute(value, axis, pairs)


def pick_pair(swapped_here, theirs, ours):
    return tuple(
        (
            jnp.where(swapped_here, other_part, mine_part)
            for other_part, mine_part in zip(theirs, ours)
        )
    )


def activate(up_pre, grad_hidden):
    up_sig = jax.nn.sigmoid(up_pre)
    hidden = (up_pre * up_sig).astype(jnp.bfloat16)
    pairing_part = jnp.sum(hidden.astype(jnp.float32) * grad_hidden, -1)
    grad_pre = (grad_hidden * up_sig * (1.0 + up_pre * (1.0 - up_sig))).astype(jnp.bfloat16)
    return (hidden, pairing_part, grad_pre)


def local(tokens, routes, logits, cotangent, pair_flags, w_up, w_down):
    devices_ex = lax.axis_size("expert")
    experts = devices_ex // 2
    half_way = experts // 2
    here_index = lax.axis_index("expert")
    slot_here = here_index // 2
    tok_rows, top_count = routes.shape
    quarter = tokens.shape[1]
    capacity = max(2, 2 * (3 * tok_rows * top_count // (4 * experts)))
    expert_ids = jnp.arange(experts, dtype=jnp.int32)
    paired = jnp.concatenate([pair_flags, pair_flags]) > 0
    owner_slot = jnp.where(paired, (expert_ids + half_way) % experts, expert_ids)
    swapped_here = paired[slot_here]
    affinity = jax.nn.sigmoid(logits)
    weights = affinity / jnp.sum(affinity, -1, keepdims=True)
    scaled = (weights[:, :, None] * cotangent[:, None, :].astype(jnp.float32)).astype(jnp.bfloat16)
    scaled = scaled.reshape(-1, quarter)
    flat_routes = routes.reshape(-1)
    onehot = (flat_routes[:, None] == expert_ids[None, :]).astype(jnp.int32)
    slot_rank = jnp.sum(jnp.cumsum(onehot, 0) * onehot, 1) - 1
    own_weights = (w_up, w_down)
    shifted = passed_along((w_up, w_down), "expert", devices_ex // 2)
    resident = pick_pair(swapped_here, shifted, own_weights)
    target = owner_slot[flat_routes]
    position = target * capacity + slot_rank
    empty_rows = jnp.zeros((experts * capacity, quarter), jnp.bfloat16)
    token_buf = (
        empty_rows.at[position]
        .set(jnp.repeat(tokens, top_count, axis=0))
        .reshape(experts, capacity, quarter)
    )
    scaled_buf = empty_rows.at[position].set(scaled).reshape(experts, capacity, quarter)
    token_in, scaled_in = (
        lax.all_to_all(
            jnp.repeat(token_buf, 2, axis=0), "expert", split_axis=0, concat_axis=0, tiled=True
        ),
        lax.all_to_all(
            jnp.repeat(scaled_buf, 2, axis=0), "expert", split_axis=0, concat_axis=0, tiled=True
        ),
    )
    routed_rows = token_in.reshape(-1, quarter)
    scaled_rows = scaled_in.reshape(-1, quarter)
    up_block, down_block = resident
    up_part = jnp.dot(routed_rows, up_block, preferred_element_type=jnp.float32)
    grad_part = jnp.dot(scaled_rows, down_block, preferred_element_type=jnp.float32)
    up_pre, grad_hidden = (
        lax.psum(up_part.astype(jnp.bfloat16), "dp").astype(jnp.float32),
        lax.psum(grad_part.astype(jnp.bfloat16), "dp").astype(jnp.float32),
    )
    hidden, pairing_part, grad_pre = activate(up_pre, grad_hidden)
    pairing_half = pairing_part.astype(jnp.bfloat16)
    route_half = jnp.einsum(
        "nf,df->nd", grad_pre, up_block, preferred_element_type=jnp.float32
    ).astype(jnp.bfloat16)
    grad_up = jnp.einsum(
        "nd,nf->df", routed_rows, grad_pre, preferred_element_type=jnp.float32
    ).astype(jnp.bfloat16)
    grad_down = jnp.einsum(
        "nd,nf->df", scaled_rows, hidden, preferred_element_type=jnp.float32
    ).astype(jnp.bfloat16)
    back_rows, back_pairing = (
        lax.all_to_all(
            route_half.reshape(devices_ex, capacity, quarter),
            "expert",
            split_axis=0,
            concat_axis=0,
            tiled=True,
        ),
        lax.all_to_all(
            pairing_half.reshape(devices_ex, capacity),
            "expert",
            split_axis=0,
            concat_axis=0,
            tiled=True,
        ),
    )
    back_grid = back_rows.reshape(experts, 2, capacity, quarter)
    picked = back_grid[target, :, slot_rank]
    grad_tokens = jnp.sum(
        picked.astype(jnp.float32).reshape(tok_rows, top_count * 2, quarter), 1
    ).astype(jnp.bfloat16)
    pair_grid = back_pairing.reshape(experts, 2, capacity)
    pair_picked = pair_grid[target, :, slot_rank]
    pairing_mine = jnp.sum(pair_picked.astype(jnp.float32), 1).reshape(tok_rows, top_count)
    grad_logits = (1.0 - affinity) * (
        pairing_mine - weights * jnp.sum(pairing_mine, -1, keepdims=True)
    )
    return (grad_tokens, grad_logits, grad_up, grad_down)

def dense(tokens, routes, logits, cotangent, pair_flags, w_up, w_down):
    devices_ex = lax.axis_size("expert")
    experts = devices_ex // 2
    half_way = experts // 2
    here_index = lax.axis_index("expert")
    dp_count = lax.axis_size("dp")
    slot_here = here_index // 2
    tok_rows, top_count = routes.shape
    expert_ids = jnp.arange(experts, dtype=jnp.int32)
    paired = jnp.concatenate([pair_flags, pair_flags]) > 0
    swapped_here = paired[slot_here]
    owner_here = jnp.where(swapped_here, (slot_here + half_way) % experts, slot_here)
    affinity = jax.nn.sigmoid(logits)
    weights = affinity / jnp.sum(affinity, -1, keepdims=True)
    chosen = (routes[:, :, None] == expert_ids[None, None, :]).astype(jnp.float32)
    spread = jnp.sum(weights[:, :, None] * chosen, 1)
    spread_all = lax.all_gather(spread, "expert", axis=0, tiled=True)
    tokens_all = lax.all_gather(tokens, "expert", axis=0, tiled=True)
    cot_all = lax.all_gather(cotangent, "expert", axis=0, tiled=True)
    cot_wide = cot_all.astype(jnp.float32)
    scaled_home = (lax.dynamic_slice_in_dim(spread_all, slot_here, 1, 1) * cot_wide).astype(jnp.bfloat16)
    scaled_slot = (lax.dynamic_slice_in_dim(spread_all, owner_here, 1, 1) * cot_wide).astype(jnp.bfloat16)
    up_part = jnp.dot(tokens_all, w_up, preferred_element_type=jnp.float32).astype(jnp.bfloat16)
    grad_part = jnp.dot(scaled_home, w_down, preferred_element_type=jnp.float32).astype(jnp.bfloat16)
    both = lax.psum_scatter(jnp.concatenate([up_part, grad_part], 1), "dp", scatter_dimension=0, tiled=True)
    up_pre, grad_hidden = jnp.split(both.astype(jnp.float32), 2, axis=1)
    hidden, pairing_part, grad_pre = activate(up_pre, grad_hidden)
    pair_all = lax.all_gather(
        pairing_part.astype(jnp.bfloat16)[None], ("expert", "dp"), axis=0, tiled=True
    )
    joined = jnp.concatenate([grad_pre, hidden], 1)
    theirs = passed_along(joined, "expert", devices_ex // 2)
    slot_joined = jnp.where(swapped_here, theirs, joined)
    gathered = lax.all_gather(jnp.concatenate([grad_pre, slot_joined], 1), "dp", axis=0, tiled=True)
    grad_home, grad_slot, hidden_slot = jnp.split(gathered, 3, axis=1)
    route_part = jnp.einsum("nf,df->nd", grad_home, w_up, preferred_element_type=jnp.float32).astype(jnp.bfloat16)
    grad_up = jnp.einsum("nd,nf->df", tokens_all, grad_slot, preferred_element_type=jnp.float32).astype(jnp.bfloat16)
    grad_down = jnp.einsum("nd,nf->df", scaled_slot, hidden_slot, preferred_element_type=jnp.float32).astype(jnp.bfloat16)
    grad_tokens = lax.psum_scatter(route_part, "expert", scatter_dimension=0, tiled=True)
    pair_grid = pair_all.reshape(experts, 2, devices_ex, tok_rows)
    pair_mine = jnp.sum(pair_grid[:, :, here_index].astype(jnp.float32), 1)
    pairing_mine = jnp.sum(chosen * pair_mine.T[:, None, :], -1)
    grad_logits = (1.0 - affinity) * (
        pairing_mine - weights * jnp.sum(pairing_mine, -1, keepdims=True)
    )
    return (grad_tokens, grad_logits, grad_up, grad_down)


def solution(mesh):
    in_specs = (
        P("expert", "dp"),
        P("expert", None),
        P("expert", None),
        P("expert", "dp"),
        P(),
        P("dp", "expert"),
        P("dp", "expert"),
    )
    body = dense if mesh.shape["expert"] <= 8 else local
    out_specs = (P("expert", "dp"), P("expert", None), P("dp", "expert"), P("dp", "expert"))
    return jax.shard_map(body, mesh=mesh, in_specs=in_specs, out_specs=out_specs, check_vma=False)
```

```python
import functools
import jax
import jax.numpy as jnp
from jax import lax
from jax.experimental import pallas as pl
from jax.experimental.pallas import tpu as pltpu
from jax.sharding import PartitionSpec as P


def passed_along(value, axis, steps):
    count = lax.axis_size(axis)
    pairs = [(source, (source + steps) % count) for source in range(count)]
    return lax.ppermute(value, axis, pairs)


def pick_pair(swapped_here, theirs, ours):
    return tuple(
        (
            jnp.where(swapped_here, other_part, mine_part)
            for other_part, mine_part in zip(theirs, ours)
        )
    )


def activate(up_pre, grad_hidden):
    up_sig = jax.nn.sigmoid(up_pre)
    hidden = (up_pre * up_sig).astype(jnp.bfloat16)
    pairing_part = jnp.sum(hidden.astype(jnp.float32) * grad_hidden, -1)
    grad_pre = (grad_hidden * up_sig * (1.0 + up_pre * (1.0 - up_sig))).astype(jnp.bfloat16)
    return (hidden, pairing_part, grad_pre)


def local(tokens, routes, logits, cotangent, pair_flags, w_up, w_down):
    devices_ex = lax.axis_size("expert")
    experts = devices_ex // 2
    half_way = experts // 2
    here_index = lax.axis_index("expert")
    slot_here = here_index // 2
    tok_rows, top_count = routes.shape
    quarter = tokens.shape[1]
    capacity = max(2, 2 * (3 * tok_rows * top_count // (4 * experts)))
    expert_ids = jnp.arange(experts, dtype=jnp.int32)
    paired = jnp.concatenate([pair_flags, pair_flags]) > 0
    owner_slot = jnp.where(paired, (expert_ids + half_way) % experts, expert_ids)
    swapped_here = paired[slot_here]
    affinity = jax.nn.sigmoid(logits)
    weights = affinity / jnp.sum(affinity, -1, keepdims=True)
    scaled = (weights[:, :, None] * cotangent[:, None, :].astype(jnp.float32)).astype(jnp.bfloat16)
    scaled = scaled.reshape(-1, quarter)
    flat_routes = routes.reshape(-1)
    onehot = (flat_routes[:, None] == expert_ids[None, :]).astype(jnp.int32)
    route_order = jnp.arange(tok_rows * top_count, dtype=jnp.int32)
    same = flat_routes[:, None] == flat_routes[None, :]
    slot_rank = jnp.sum((same & (route_order[None, :] < route_order[:, None])).astype(jnp.int32), 1)
    own_weights = (w_up, w_down)
    shifted = passed_along((w_up, w_down), "expert", devices_ex // 2)
    resident = pick_pair(swapped_here, shifted, own_weights)
    target = owner_slot[flat_routes]
    position = target * capacity + slot_rank
    empty_rows = jnp.zeros((experts * capacity, quarter), jnp.bfloat16)
    token_buf = (
        empty_rows.at[position]
        .set(jnp.repeat(tokens, top_count, axis=0))
        .reshape(experts, capacity, quarter)
    )
    scaled_buf = empty_rows.at[position].set(scaled).reshape(experts, capacity, quarter)
    token_in, scaled_in = (
        lax.all_to_all(
            jnp.repeat(token_buf, 2, axis=0), "expert", split_axis=0, concat_axis=0, tiled=True
        ),
        lax.all_to_all(
            jnp.repeat(scaled_buf, 2, axis=0), "expert", split_axis=0, concat_axis=0, tiled=True
        ),
    )
    routed_rows = token_in.reshape(-1, quarter)
    scaled_rows = scaled_in.reshape(-1, quarter)
    up_block, down_block = resident
    up_part = jnp.dot(routed_rows, up_block, preferred_element_type=jnp.float32)
    grad_part = jnp.dot(scaled_rows, down_block, preferred_element_type=jnp.float32)
    up_pre, grad_hidden = (
        lax.psum(up_part.astype(jnp.bfloat16), "dp").astype(jnp.float32),
        lax.psum(grad_part.astype(jnp.bfloat16), "dp").astype(jnp.float32),
    )
    hidden, pairing_part, grad_pre = activate(up_pre, grad_hidden)
    pairing_half = pairing_part.astype(jnp.bfloat16)
    route_half = jnp.einsum(
        "nf,df->nd", grad_pre, up_block, preferred_element_type=jnp.float32
    ).astype(jnp.bfloat16)
    grad_up = jnp.einsum(
        "nd,nf->df", routed_rows, grad_pre, preferred_element_type=jnp.float32
    ).astype(jnp.bfloat16)
    grad_down = jnp.einsum(
        "nd,nf->df", scaled_rows, hidden, preferred_element_type=jnp.float32
    ).astype(jnp.bfloat16)
    back_rows, back_pairing = (
        lax.all_to_all(
            route_half.reshape(devices_ex, capacity, quarter),
            "expert",
            split_axis=0,
            concat_axis=0,
            tiled=True,
        ),
        lax.all_to_all(
            pairing_half.reshape(devices_ex, capacity),
            "expert",
            split_axis=0,
            concat_axis=0,
            tiled=True,
        ),
    )
    back_grid = back_rows.reshape(experts, 2, capacity, quarter)
    picked = [
        back_grid[:, half].reshape(-1, quarter)[position].astype(jnp.float32) for half in range(2)
    ]
    grad_tokens = jnp.sum(
        (picked[0] + picked[1]).reshape(tok_rows, top_count, quarter), 1
    ).astype(jnp.bfloat16)
    pair_grid = back_pairing.reshape(experts, 2, capacity)
    pair_picked = pair_grid[target, :, slot_rank]
    pairing_mine = jnp.sum(pair_picked.astype(jnp.float32), 1).reshape(tok_rows, top_count)
    grad_logits = (1.0 - affinity) * (
        pairing_mine - weights * jnp.sum(pairing_mine, -1, keepdims=True)
    )
    return (grad_tokens, grad_logits, grad_up, grad_down)

def everything(
    zs, dps, tok_ref, cot_ref, spread_ref, home_ref, slot_ref, swap_ref, up_ref, down_ref,
    gt_ref, pair_ref, gu_ref, gd_ref,
    rows_all, scaled_slot, part, part_in, mine, theirs, home_g, slot_g, back, back_x, back_z, to_z,
    row_s, row_r, rs_s, rs_r, gh_s, gh_r, home_s, home_r, slot_s, slot_r, bx_s, bx_r, bz_s, bz_r,
):
    me = lax.axis_index("expert")
    d = lax.axis_index("dp")
    z, x = me // 2, me % 2
    other = z * 2 + 1 - x
    partner = ((z + zs // 2) % zs) * 2 + x
    quarter = tok_ref.shape[1]
    ff = up_ref.shape[1]
    bf, f32 = jnp.bfloat16, jnp.float32

    def remote(src, dst, send, recv, expert, dp):
        return pltpu.make_async_remote_copy(
            src_ref=src, dst_ref=dst, send_sem=send, recv_sem=recv,
            device_id={"expert": expert, "dp": dp}, device_id_type=pl.DeviceIdType.MESH,
        )

    def peer(r):
        return lax.rem(d + r, dps)

    barrier = pltpu.get_barrier_semaphore()
    for r in range(1, zs):
        pl.semaphore_signal(
            barrier, inc=1, device_id={"expert": ((z + r) % zs) * 2 + x, "dp": d},
            device_id_type=pl.DeviceIdType.MESH,
        )
    pl.semaphore_signal(
        barrier, inc=1, device_id={"expert": other, "dp": d}, device_id_type=pl.DeviceIdType.MESH
    )
    for r in range(1, dps):
        pl.semaphore_signal(
            barrier, inc=1, device_id={"expert": me, "dp": peer(r)},
            device_id_type=pl.DeviceIdType.MESH,
        )
    rows_all[me, :, 0:quarter] = tok_ref[...]
    rows_all[me, :, quarter : 2 * quarter] = cot_ref[...]
    lanes = lax.broadcasted_iota(jnp.int32, spread_ref.shape, 1)
    whole = spread_ref[...]
    high = whole.astype(bf).astype(f32)
    middle = (whole - high).astype(bf).astype(f32)
    low = whole - high - middle
    terms = jnp.where(lanes < 32, high, jnp.where(lanes < 64, middle, low))
    rows_all[me, :, 2 * quarter :] = terms.astype(bf)
    pl.semaphore_wait(barrier, zs - 1 + 1 + dps - 1)

    def row_copy(b, way, expert):
        return remote(
            rows_all.at[b], rows_all.at[b], row_s.at[b, way], row_r.at[b], expert, d
        )

    def rs_copy(b, r):
        return remote(
            part.at[b, peer(r)], part_in.at[b, d], rs_s.at[b, r - 1], rs_r.at[b, d], me, peer(r)
        )

    def gh_copy(b):
        return remote(mine.at[b], theirs.at[b], gh_s.at[b], gh_r.at[b], partner, d)

    def home_copy(b, r):
        return remote(
            home_g.at[b, d], home_g.at[b, d], home_s.at[b, r - 1], home_r.at[b, d], me, peer(r)
        )

    def slot_copy(b, r):
        return remote(
            slot_g.at[b, d], slot_g.at[b, d], slot_s.at[b, r - 1], slot_r.at[b, d], me, peer(r)
        )

    def zz_of(j):
        far = (j + 1) // 2
        return jnp.where(j % 2 == 1, z + far, z - far)

    def valid(j):
        zz = zz_of(j)
        return (j >= 0) & (j < 2 * zs - 1) & (zz >= 0) & (zz < zs)

    def multiply(b):
        ext = rows_all[b, :, 2 * quarter :].astype(f32)
        cot = rows_all[b, :, quarter : 2 * quarter].astype(f32)
        w_home = jnp.sum(ext * home_ref[...], axis=1, keepdims=True)
        w_slot = jnp.sum(ext * slot_ref[...], axis=1, keepdims=True)
        up = jnp.dot(rows_all[b, :, 0:quarter], up_ref[...], preferred_element_type=f32)
        part[b, :, :, 0:ff] = up.astype(bf).reshape(dps, -1, ff)
        scaled = (w_home * cot).astype(bf)
        grad = jnp.dot(scaled, down_ref[...], preferred_element_type=f32)
        part[b, :, :, ff:] = grad.astype(bf).reshape(dps, -1, ff)
        for r in range(1, dps):
            rs_copy(b, r).start()
        scaled_slot[b] = (w_slot * cot).astype(bf)

    def act(b):
        for r in range(1, dps):
            remote(
                part.at[b, peer(r)], part_in.at[b, peer(r)], rs_s.at[b, r - 1],
                rs_r.at[b, peer(r)], me, peer(r),
            ).wait_recv()
        total = part[b, d].astype(f32)
        for r in range(1, dps):
            total = total + part_in[b, peer(r)].astype(f32)
        hidden, pairing, grad_pre = activate(total[:, 0:ff], total[:, ff:])
        mine[b, :, 0:ff] = grad_pre
        mine[b, :, ff:] = hidden
        gh_copy(b).start()
        at = lax.broadcasted_iota(jnp.int32, (grad_pre.shape[0], 128), 1)
        home_g[b, d, :, 0:ff] = grad_pre
        home_g[b, d, :, ff:] = jnp.where(at == z, pairing[:, None], 0.0).astype(bf)
        for r in range(1, dps):
            home_copy(b, r).start()

    def first(j, _):
        zz = zz_of(j)

        @pl.when(valid(j))
        def _():
            b = zz * 2 + x

            @pl.when(j > 0)
            def _():
                row_copy(b, 0, me).wait_recv()

            @pl.when((zz <= z) & (z < zs - 1))
            def _():
                row_copy(b, 0, me + 2).start()

            @pl.when((zz >= z) & (z > 0))
            def _():
                row_copy(b, 1, me - 2).start()

            row_copy(b, 2, other).start()
            multiply(b)

        @pl.when(valid(j - 1))
        def _():
            b = zz_of(j - 1) * 2 + 1 - x
            row_copy(b, 2, other).wait_recv()
            multiply(b)
            act(zz_of(j - 1) * 2 + x)

        @pl.when(valid(j - 2))
        def _():
            act(zz_of(j - 2) * 2 + 1 - x)

        return 0

    lax.fori_loop(0, 2 * zs + 1, first, 0)

    def second(j, _):
        @pl.when(valid(j))
        def _():
            for side in range(2):
                b = ((zz_of(j) + zs // 2) % zs) * 2 + side
                gh_copy(b).wait_recv()
                swap = swap_ref[...]
                picked = mine[b].astype(f32) * (1.0 - swap) + theirs[b].astype(f32) * swap
                slot_g[b, d] = picked.astype(bf)
                for r in range(1, dps):
                    slot_copy(b, r).start()

        return 0

    lax.fori_loop(0, 2 * zs - 1, second, 0)

    def back_rows(b):
        for r in range(1, dps):
            remote(
                home_g.at[b, d], home_g.at[b, peer(r)], home_s.at[b, r - 1],
                home_r.at[b, peer(r)], me, peer(r),
            ).wait_recv()
        joined = home_g[b].reshape(-1, ff + 128)
        rows = lax.dot_general(
            joined[:, 0:ff], up_ref[...], (((1,), (1,)), ((), ())), preferred_element_type=f32
        )
        back[b, :, 0:quarter] = rows.astype(bf)
        back[b, :, quarter:] = joined[:, ff:]

    def bx_copy(zz):
        return remote(
            back.at[zz * 2 + 1 - x], back_x.at[zz], bx_s.at[zz], bx_r.at[zz], other, d
        )

    def bz_copy(zz):
        return remote(to_z.at[zz], back_z.at[z], bz_s.at[zz], bz_r.at[z], zz * 2 + x, d)

    def third(r, _):
        zz = (z + r) % zs
        back_rows(zz * 2 + 1 - x)
        bx_copy(zz).start()
        return 0

    lax.fori_loop(1, zs + 1, third, 0)

    def fourth(r, _):
        zz = (z + r) % zs
        b = zz * 2 + x
        back_rows(b)
        bx_copy(zz).wait_recv()
        both = (back[b].astype(f32) + back_x[zz].astype(f32)).astype(bf)

        @pl.when(zz != z)
        def _():
            to_z[zz] = both
            bz_copy(zz).start()

        @pl.when(zz == z)
        def _():
            back_z[z] = both

        return 0

    lax.fori_loop(1, zs + 1, fourth, 0)

    def slot_wait(b, _):
        for r in range(1, dps):
            remote(
                slot_g.at[b, d], slot_g.at[b, peer(r)], slot_s.at[b, r - 1],
                slot_r.at[b, peer(r)], me, peer(r),
            ).wait_recv()
        return 0

    lax.fori_loop(0, 2 * zs, slot_wait, 0)

    def weight_grads(c, _):
        at = pl.ds(pl.multiple_of(c * 128, 128), 128)
        tokens = rows_all[:, :, at].reshape(-1, 128)
        gu_ref[at, :] = lax.dot_general(
            tokens, slot_g[:, :, :, 0:ff].reshape(-1, ff), (((0,), (0,)), ((), ())),
            preferred_element_type=f32,
        ).astype(bf)
        scaled = scaled_slot[:, :, at].reshape(-1, 128)
        gd_ref[at, :] = lax.dot_general(
            scaled, slot_g[:, :, :, ff:].reshape(-1, ff), (((0,), (0,)), ((), ())),
            preferred_element_type=f32,
        ).astype(bf)
        return 0

    lax.fori_loop(0, quarter // 128, weight_grads, 0)

    for r in range(1, zs):
        zz = (z + r) % zs
        remote(to_z.at[zz], back_z.at[zz], bz_s.at[zz], bz_r.at[zz], zz * 2 + x, d).wait_recv()
    total = back_z[0].astype(f32)
    for r in range(1, zs):
        total = total + back_z[r].astype(f32)
    gt_ref[...] = total[:, 0:quarter].astype(bf)
    pair_ref[...] = total[:, quarter:]

    def drain(b, _):
        zz = b // 2

        @pl.when(b % 2 == x)
        def _():
            @pl.when((zz <= z) & (z < zs - 1))
            def _():
                row_copy(b, 0, me + 2).wait_send()

            @pl.when((zz >= z) & (z > 0))
            def _():
                row_copy(b, 1, me - 2).wait_send()

            row_copy(b, 2, other).wait_send()

            @pl.when(zz != z)
            def _():
                bz_copy(zz).wait_send()

            bx_copy(zz).wait_send()

        for r in range(1, dps):
            rs_copy(b, r).wait_send()
            home_copy(b, r).wait_send()
            slot_copy(b, r).wait_send()
        gh_copy(b).wait_send()
        return 0

    lax.fori_loop(0, 2 * zs, drain, 0)


def one_kernel(tokens, routes, logits, cotangent, pair_flags, w_up, w_down):
    devices_ex = lax.axis_size("expert")
    dps = lax.axis_size("dp")
    experts = devices_ex // 2
    half_way = experts // 2
    slot_here = lax.axis_index("expert") // 2
    tok_rows, top_count = routes.shape
    quarter = tokens.shape[1]
    ff = w_up.shape[1]
    expert_ids = jnp.arange(experts, dtype=jnp.int32)
    paired = jnp.concatenate([pair_flags, pair_flags]) > 0
    swapped_here = paired[slot_here]
    owner_here = jnp.where(swapped_here, (slot_here + half_way) % experts, slot_here)
    affinity = jax.nn.sigmoid(logits)
    weights = affinity / jnp.sum(affinity, -1, keepdims=True)
    lanes = jnp.arange(128, dtype=jnp.int32)
    group = jnp.where(lanes < 96, lanes % 32, 32)
    spread = jnp.zeros((tok_rows, 128), jnp.float32)
    for k in range(top_count):
        spread = spread + jnp.where(routes[:, k : k + 1] == group[None, :], weights[:, k : k + 1], 0.0)
    pick_home = (group == slot_here).astype(jnp.float32)[None, :]
    pick_slot = (group == owner_here).astype(jnp.float32)[None, :]
    swap = jnp.broadcast_to(swapped_here.astype(jnp.float32), (1, 2 * ff))
    bf = jnp.bfloat16
    part_rows = tok_rows // dps
    vmem = pl.BlockSpec(memory_space=pltpu.VMEM)
    dma = pltpu.SemaphoreType.DMA
    n = devices_ex
    grad_tokens, pairs, grad_up, grad_down = pl.pallas_call(
        functools.partial(everything, experts, dps),
        out_shape=(
            jax.ShapeDtypeStruct((tok_rows, quarter), bf),
            jax.ShapeDtypeStruct((tok_rows, 128), jnp.float32),
            jax.ShapeDtypeStruct((quarter, ff), bf),
            jax.ShapeDtypeStruct((quarter, ff), bf),
        ),
        in_specs=[vmem] * 8,
        out_specs=(vmem,) * 4,
        scratch_shapes=[
            pltpu.VMEM((n, tok_rows, 2 * quarter + 128), bf),
            pltpu.VMEM((n, tok_rows, quarter), bf),
            pltpu.VMEM((n, dps, part_rows, 2 * ff), bf),
            pltpu.VMEM((n, dps, part_rows, 2 * ff), bf),
            pltpu.VMEM((n, part_rows, 2 * ff), bf),
            pltpu.VMEM((n, part_rows, 2 * ff), bf),
            pltpu.VMEM((n, dps, part_rows, ff + 128), bf),
            pltpu.VMEM((n, dps, part_rows, 2 * ff), bf),
            pltpu.VMEM((n, tok_rows, quarter + 128), bf),
            pltpu.VMEM((experts, tok_rows, quarter + 128), bf),
            pltpu.VMEM((experts, tok_rows, quarter + 128), bf),
            pltpu.VMEM((experts, tok_rows, quarter + 128), bf),
            dma((n, 3)), dma((n,)),
            dma((n, dps - 1)), dma((n, dps)),
            dma((n,)), dma((n,)),
            dma((n, dps - 1)), dma((n, dps)),
            dma((n, dps - 1)), dma((n, dps)),
            dma((experts,)), dma((experts,)),
            dma((experts,)), dma((experts,)),
        ],
        compiler_params=pltpu.CompilerParams(
            collective_id=0, has_side_effects=True, vmem_limit_bytes=56 * 1024 * 1024
        ),
    )(tokens, cotangent, spread, pick_home, pick_slot, swap, w_up, w_down)
    chosen = (routes[:, :, None] == expert_ids[None, None, :]).astype(jnp.float32)
    pairing_mine = jnp.sum(chosen * pairs[:, None, 0:experts], -1)
    grad_logits = (1.0 - affinity) * (
        pairing_mine - weights * jnp.sum(pairing_mine, -1, keepdims=True)
    )
    return (grad_tokens, grad_logits, grad_up, grad_down)


def solution(mesh):
    in_specs = (
        P("expert", "dp"),
        P("expert", None),
        P("expert", None),
        P("expert", "dp"),
        P(),
        P("dp", "expert"),
        P("dp", "expert"),
    )
    body = one_kernel if mesh.shape["expert"] <= 8 else local
    out_specs = (P("expert", "dp"), P("expert", None), P("dp", "expert"), P("dp", "expert"))
    return jax.shard_map(body, mesh=mesh, in_specs=in_specs, out_specs=out_specs, check_vma=False)
```

```python
import functools
import jax
import jax.numpy as jnp
from jax import lax
from jax.experimental import pallas as pl
from jax.experimental.pallas import tpu as pltpu
from jax.sharding import PartitionSpec as P


def passed_along(value, axis, steps):
    count = lax.axis_size(axis)
    pairs = [(source, (source + steps) % count) for source in range(count)]
    return lax.ppermute(value, axis, pairs)


def pick_pair(swapped_here, theirs, ours):
    return tuple(
        (
            jnp.where(swapped_here, other_part, mine_part)
            for other_part, mine_part in zip(theirs, ours)
        )
    )


def activate(up_pre, grad_hidden):
    up_sig = jax.nn.sigmoid(up_pre)
    hidden = (up_pre * up_sig).astype(jnp.bfloat16)
    pairing_part = jnp.sum(hidden.astype(jnp.float32) * grad_hidden, -1)
    grad_pre = (grad_hidden * up_sig * (1.0 + up_pre * (1.0 - up_sig))).astype(jnp.bfloat16)
    return (hidden, pairing_part, grad_pre)


def local(tokens, routes, logits, cotangent, pair_flags, w_up, w_down):
    devices_ex = lax.axis_size("expert")
    experts = devices_ex // 2
    half_way = experts // 2
    here_index = lax.axis_index("expert")
    slot_here = here_index // 2
    tok_rows, top_count = routes.shape
    quarter = tokens.shape[1]
    capacity = max(2, 2 * (3 * tok_rows * top_count // (4 * experts)))
    expert_ids = jnp.arange(experts, dtype=jnp.int32)
    paired = jnp.concatenate([pair_flags, pair_flags]) > 0
    owner_slot = jnp.where(paired, (expert_ids + half_way) % experts, expert_ids)
    swapped_here = paired[slot_here]
    affinity = jax.nn.sigmoid(logits)
    weights = affinity / jnp.sum(affinity, -1, keepdims=True)
    scaled = (weights[:, :, None] * cotangent[:, None, :].astype(jnp.float32)).astype(jnp.bfloat16)
    scaled = scaled.reshape(-1, quarter)
    flat_routes = routes.reshape(-1)
    onehot = (flat_routes[:, None] == expert_ids[None, :]).astype(jnp.int32)
    route_order = jnp.arange(tok_rows * top_count, dtype=jnp.int32)
    same = flat_routes[:, None] == flat_routes[None, :]
    slot_rank = jnp.sum((same & (route_order[None, :] < route_order[:, None])).astype(jnp.int32), 1)
    own_weights = (w_up, w_down)
    shifted = passed_along((w_up, w_down), "expert", devices_ex // 2)
    resident = pick_pair(swapped_here, shifted, own_weights)
    target = owner_slot[flat_routes]
    position = target * capacity + slot_rank
    empty_rows = jnp.zeros((experts * capacity, quarter), jnp.bfloat16)
    token_buf = (
        empty_rows.at[position]
        .set(jnp.repeat(tokens, top_count, axis=0))
        .reshape(experts, capacity, quarter)
    )
    scaled_buf = empty_rows.at[position].set(scaled).reshape(experts, capacity, quarter)
    token_in, scaled_in = (
        lax.all_to_all(
            jnp.repeat(token_buf, 2, axis=0), "expert", split_axis=0, concat_axis=0, tiled=True
        ),
        lax.all_to_all(
            jnp.repeat(scaled_buf, 2, axis=0), "expert", split_axis=0, concat_axis=0, tiled=True
        ),
    )
    routed_rows = token_in.reshape(-1, quarter)
    scaled_rows = scaled_in.reshape(-1, quarter)
    up_block, down_block = resident
    up_part = jnp.dot(routed_rows, up_block, preferred_element_type=jnp.float32)
    grad_part = jnp.dot(scaled_rows, down_block, preferred_element_type=jnp.float32)
    up_pre, grad_hidden = (
        lax.psum(up_part.astype(jnp.bfloat16), "dp").astype(jnp.float32),
        lax.psum(grad_part.astype(jnp.bfloat16), "dp").astype(jnp.float32),
    )
    hidden, pairing_part, grad_pre = activate(up_pre, grad_hidden)
    pairing_half = pairing_part.astype(jnp.bfloat16)
    route_half = jnp.einsum(
        "nf,df->nd", grad_pre, up_block, preferred_element_type=jnp.float32
    ).astype(jnp.bfloat16)
    grad_up = jnp.einsum(
        "nd,nf->df", routed_rows, grad_pre, preferred_element_type=jnp.float32
    ).astype(jnp.bfloat16)
    grad_down = jnp.einsum(
        "nd,nf->df", scaled_rows, hidden, preferred_element_type=jnp.float32
    ).astype(jnp.bfloat16)
    back_rows, back_pairing = (
        lax.all_to_all(
            route_half.reshape(devices_ex, capacity, quarter),
            "expert",
            split_axis=0,
            concat_axis=0,
            tiled=True,
        ),
        lax.all_to_all(
            pairing_half.reshape(devices_ex, capacity),
            "expert",
            split_axis=0,
            concat_axis=0,
            tiled=True,
        ),
    )
    back_grid = back_rows.reshape(experts, 2, capacity, quarter)
    picked = [
        back_grid[:, half].reshape(-1, quarter)[position].astype(jnp.float32) for half in range(2)
    ]
    grad_tokens = jnp.sum(
        (picked[0] + picked[1]).reshape(tok_rows, top_count, quarter), 1
    ).astype(jnp.bfloat16)
    pair_grid = back_pairing.reshape(experts, 2, capacity)
    pair_picked = pair_grid[target, :, slot_rank]
    pairing_mine = jnp.sum(pair_picked.astype(jnp.float32), 1).reshape(tok_rows, top_count)
    grad_logits = (1.0 - affinity) * (
        pairing_mine - weights * jnp.sum(pairing_mine, -1, keepdims=True)
    )
    return (grad_tokens, grad_logits, grad_up, grad_down)

def everything(
    zs, dps, tok_ref, cot_ref, routes_ref, logits_ref, flags_ref, up_hbm, down_hbm,
    gt_ref, gl_ref, gu_ref, gd_ref,
    up_ref, down_ref,
    rows_all, scaled_slot, part, part_in, mine, theirs, home_g, slot_g, back, back_x, back_z, to_z,
    row_s, row_r, rs_s, rs_r, gh_s, gh_r, home_s, home_r, slot_s, slot_r, bx_s, bx_r, bz_s, bz_r, local_s,
):
    me = lax.axis_index("expert")
    d = lax.axis_index("dp")
    z, x = me // 2, me % 2
    other = z * 2 + 1 - x
    partner = ((z + zs // 2) % zs) * 2 + x
    quarter = tok_ref.shape[1]
    ff = up_ref.shape[1]
    bf, f32 = jnp.bfloat16, jnp.float32

    def remote(src, dst, send, recv, expert, dp):
        return pltpu.make_async_remote_copy(
            src_ref=src, dst_ref=dst, send_sem=send, recv_sem=recv,
            device_id={"expert": expert, "dp": dp}, device_id_type=pl.DeviceIdType.MESH,
        )

    def peer(r):
        return lax.rem(d + r, dps)

    barrier = pltpu.get_barrier_semaphore()
    for r in range(1, zs):
        pl.semaphore_signal(
            barrier, inc=1, device_id={"expert": ((z + r) % zs) * 2 + x, "dp": d},
            device_id_type=pl.DeviceIdType.MESH,
        )
    pl.semaphore_signal(
        barrier, inc=1, device_id={"expert": other, "dp": d}, device_id_type=pl.DeviceIdType.MESH
    )
    for r in range(1, dps):
        pl.semaphore_signal(
            barrier, inc=1, device_id={"expert": me, "dp": peer(r)},
            device_id_type=pl.DeviceIdType.MESH,
        )
    held = [
        pltpu.make_async_copy(tok_ref, rows_all.at[me, :, 0:quarter], local_s.at[0]),
        pltpu.make_async_copy(cot_ref, rows_all.at[me, :, quarter : 2 * quarter], local_s.at[1]),
        pltpu.make_async_copy(up_hbm, up_ref, local_s.at[2]),
        pltpu.make_async_copy(down_hbm, down_ref, local_s.at[3]),
    ]
    for copy in held:
        copy.start()
    affinity = jax.nn.sigmoid(logits_ref[...])
    weights = affinity / jnp.sum(affinity, -1, keepdims=True)
    lanes = lax.broadcasted_iota(jnp.int32, (tok_ref.shape[0], 128), 1)
    group = jnp.where(lanes < 96, lanes % 32, 32)
    tops = logits_ref.shape[1]
    whole = jnp.zeros(lanes.shape, f32)
    for k in range(tops):
        whole = whole + jnp.where(routes_ref[:, k : k + 1] == group, weights[:, k : k + 1], 0.0)
    pair_lane = lax.broadcasted_iota(jnp.int32, flags_ref.shape, 1)
    swap = jnp.sum(
        jnp.where((pair_lane == z % (zs // 2)) & (flags_ref[...] > 0), 1.0, 0.0), 1, keepdims=True
    )
    group_row = group[0:1, :]
    pick_home = jnp.where(group_row == z, 1.0, 0.0)
    pick_far = jnp.where(group_row == (z + zs // 2) % zs, 1.0, 0.0)
    pick_slot = pick_home * (1.0 - swap) + pick_far * swap
    high = whole.astype(bf).astype(f32)
    middle = (whole - high).astype(bf).astype(f32)
    low = whole - high - middle
    terms = jnp.where(lanes < 32, high, jnp.where(lanes < 64, middle, low))
    rows_all[me, :, 2 * quarter :] = terms.astype(bf)
    for copy in held:
        copy.wait()
    pl.semaphore_wait(barrier, zs - 1 + 1 + dps - 1)

    def row_copy(b, way, expert):
        return remote(
            rows_all.at[b], rows_all.at[b], row_s.at[b, way], row_r.at[b], expert, d
        )

    def rs_copy(b, r):
        return remote(
            part.at[b, peer(r)], part_in.at[b, d], rs_s.at[b, r - 1], rs_r.at[b, d], me, peer(r)
        )

    def gh_copy(b):
        return remote(mine.at[b], theirs.at[b], gh_s.at[b], gh_r.at[b], partner, d)

    def home_copy(b, r):
        return remote(
            home_g.at[b, d], home_g.at[b, d], home_s.at[b, r - 1], home_r.at[b, d], me, peer(r)
        )

    core = d + 1 - 2 * (d % 2)
    across = (d + 2) % 4
    corner = (core + 2) % 4

    def slot_copy(b, way):
        piece = across if way == 2 else d
        target = across if way == 1 else core
        return remote(
            slot_g.at[b, piece], slot_g.at[b, piece], slot_s.at[b, way], slot_r.at[b, piece],
            me, target,
        )

    def slot_wait(b, piece, source):
        remote(
            slot_g.at[b, d], slot_g.at[b, piece], slot_s.at[b, 0], slot_r.at[b, piece], me, source
        ).wait_recv()

    def zz_of(j):
        far = (j + 1) // 2
        return jnp.where(j % 2 == 1, z + far, z - far)

    def valid(j):
        zz = zz_of(j)
        return (j >= 0) & (j < 2 * zs - 1) & (zz >= 0) & (zz < zs)

    def multiply(b):
        ext = rows_all[b, :, 2 * quarter :].astype(f32)
        cot = rows_all[b, :, quarter : 2 * quarter].astype(f32)
        w_home = jnp.sum(ext * pick_home, axis=1, keepdims=True)
        w_slot = jnp.sum(ext * pick_slot, axis=1, keepdims=True)
        up = jnp.dot(rows_all[b, :, 0:quarter], up_ref[...], preferred_element_type=f32)
        part[b, :, :, 0:ff] = up.astype(bf).reshape(dps, -1, ff)
        scaled = (w_home * cot).astype(bf)
        grad = jnp.dot(scaled, down_ref[...], preferred_element_type=f32)
        part[b, :, :, ff:] = grad.astype(bf).reshape(dps, -1, ff)
        for r in range(1, dps):
            rs_copy(b, r).start()
        scaled_slot[b] = (w_slot * cot).astype(bf)

    def act(b):
        for r in range(1, dps):
            remote(
                part.at[b, peer(r)], part_in.at[b, peer(r)], rs_s.at[b, r - 1],
                rs_r.at[b, peer(r)], me, peer(r),
            ).wait_recv()
        total = part[b, d].astype(f32)
        for r in range(1, dps):
            total = total + part_in[b, peer(r)].astype(f32)
        hidden, pairing, grad_pre = activate(total[:, 0:ff], total[:, ff:])
        mine[b, :, 0:ff] = grad_pre
        mine[b, :, ff:] = hidden
        gh_copy(b).start()
        at = lax.broadcasted_iota(jnp.int32, (grad_pre.shape[0], 128), 1)
        home_g[b, d, :, 0:ff] = grad_pre
        home_g[b, d, :, ff:] = jnp.where(at == z, pairing[:, None], 0.0).astype(bf)
        for r in range(1, dps):
            home_copy(b, r).start()

    def back_rows(b):
        for r in range(1, dps):
            remote(
                home_g.at[b, d], home_g.at[b, peer(r)], home_s.at[b, r - 1],
                home_r.at[b, peer(r)], me, peer(r),
            ).wait_recv()
        joined = home_g[b].reshape(-1, ff + 128)
        rows = lax.dot_general(
            joined[:, 0:ff], up_ref[...], (((1,), (1,)), ((), ())), preferred_element_type=f32
        )
        back[b, :, 0:quarter] = rows.astype(bf)
        back[b, :, quarter:] = joined[:, ff:]

    def bx_copy(zz):
        return remote(
            back.at[zz * 2 + 1 - x], back_x.at[zz], bx_s.at[zz], bx_r.at[zz], other, d
        )

    def bz_copy(zz):
        return remote(to_z.at[zz], back_z.at[z], bz_s.at[zz], bz_r.at[z], zz * 2 + x, d)

    def first(j, _):
        zz = zz_of(j)

        @pl.when(valid(j))
        def _():
            b = zz * 2 + x

            @pl.when(j > 0)
            def _():
                row_copy(b, 0, me).wait_recv()

            @pl.when((zz <= z) & (z < zs - 1))
            def _():
                row_copy(b, 0, me + 2).start()

            @pl.when((zz >= z) & (z > 0))
            def _():
                row_copy(b, 1, me - 2).start()

            row_copy(b, 2, other).start()
            multiply(b)

        @pl.when(valid(j - 1))
        def _():
            b = zz_of(j - 1) * 2 + 1 - x
            row_copy(b, 2, other).wait_recv()
            multiply(b)
            act(zz_of(j - 1) * 2 + x)

        @pl.when(valid(j - 2))
        def _():
            act(zz_of(j - 2) * 2 + 1 - x)
            back_rows(zz_of(j - 2) * 2 + x)

        @pl.when(valid(j - 3))
        def _():
            back_rows(zz_of(j - 3) * 2 + 1 - x)
            bx_copy(zz_of(j - 3)).start()

        return 0

    lax.fori_loop(0, 2 * zs + 2, first, 0)

    def slot_forward(b):
        slot_wait(b, across, across)
        slot_copy(b, 2).start()

    def second(j, _):
        @pl.when(valid(j))
        def _():
            for side in range(2):
                b = ((zz_of(j) + zs // 2) % zs) * 2 + side
                gh_copy(b).wait_recv()
                picked = mine[b].astype(f32) * (1.0 - swap) + theirs[b].astype(f32) * swap
                slot_g[b, d] = picked.astype(bf)
                slot_copy(b, 1).start()
                slot_copy(b, 0).start()

        @pl.when(valid(j - 1))
        def _():
            for side in range(2):
                slot_forward(((zz_of(j - 1) + zs // 2) % zs) * 2 + side)

        return 0

    lax.fori_loop(0, 2 * zs, second, 0)

    def fourth(j, _):
        zz = zz_of(j)
        b = zz * 2 + x

        @pl.when(valid(j))
        def _():
            bx_copy(zz).wait_recv()

        @pl.when(valid(j) & (zz != z))
        def _():
            to_z[zz] = (back[b].astype(f32) + back_x[zz].astype(f32)).astype(bf)
            bz_copy(zz).start()

        @pl.when(valid(j) & (zz == z))
        def _():
            back_z[z] = (back[b].astype(f32) + back_x[zz].astype(f32)).astype(bf)

        return 0

    lax.fori_loop(0, 2 * zs - 1, fourth, 0)

    def slot_rest(b, _):
        slot_wait(b, core, core)
        slot_wait(b, corner, core)
        return 0

    lax.fori_loop(0, 2 * zs, slot_rest, 0)

    def weight_grads(c, _):
        at = pl.ds(pl.multiple_of(c * 128, 128), 128)
        tokens = rows_all[:, :, at].reshape(-1, 128)
        gu_ref[at, :] = lax.dot_general(
            tokens, slot_g[:, :, :, 0:ff].reshape(-1, ff), (((0,), (0,)), ((), ())),
            preferred_element_type=f32,
        ).astype(bf)
        scaled = scaled_slot[:, :, at].reshape(-1, 128)
        gd_ref[at, :] = lax.dot_general(
            scaled, slot_g[:, :, :, ff:].reshape(-1, ff), (((0,), (0,)), ((), ())),
            preferred_element_type=f32,
        ).astype(bf)
        return 0

    lax.fori_loop(0, quarter // 128, weight_grads, 0)

    for r in range(1, zs):
        zz = (z + r) % zs
        remote(to_z.at[zz], back_z.at[zz], bz_s.at[zz], bz_r.at[zz], zz * 2 + x, d).wait_recv()
    total = back_z[0].astype(f32)
    for r in range(1, zs):
        total = total + back_z[r].astype(f32)
    gt_ref[...] = total[:, 0:quarter].astype(bf)
    pairs = total[:, quarter:]
    pairing = [
        jnp.sum(jnp.where(lanes == routes_ref[:, k : k + 1], pairs, 0.0), 1, keepdims=True)
        for k in range(tops)
    ]
    across_k = sum(pairing[1:], pairing[0])
    for k in range(tops):
        gl_ref[:, k : k + 1] = (1.0 - affinity[:, k : k + 1]) * (
            pairing[k] - weights[:, k : k + 1] * across_k
        )

    def drain(b, _):
        zz = b // 2

        @pl.when(b % 2 == x)
        def _():
            @pl.when((zz <= z) & (z < zs - 1))
            def _():
                row_copy(b, 0, me + 2).wait_send()

            @pl.when((zz >= z) & (z > 0))
            def _():
                row_copy(b, 1, me - 2).wait_send()

            row_copy(b, 2, other).wait_send()

            @pl.when(zz != z)
            def _():
                bz_copy(zz).wait_send()

            bx_copy(zz).wait_send()

        for r in range(1, dps):
            rs_copy(b, r).wait_send()
            home_copy(b, r).wait_send()
            slot_copy(b, r - 1).wait_send()
        gh_copy(b).wait_send()
        return 0

    lax.fori_loop(0, 2 * zs, drain, 0)


def one_kernel(tokens, routes, logits, cotangent, pair_flags, w_up, w_down):
    devices_ex = lax.axis_size("expert")
    dps = lax.axis_size("dp")
    experts = devices_ex // 2
    tok_rows = routes.shape[0]
    quarter = tokens.shape[1]
    ff = w_up.shape[1]
    bf = jnp.bfloat16
    part_rows = tok_rows // dps
    vmem = pl.BlockSpec(memory_space=pltpu.VMEM)
    hbm = pl.BlockSpec(memory_space=pl.ANY)
    dma = pltpu.SemaphoreType.DMA
    n = devices_ex
    return pl.pallas_call(
        functools.partial(everything, experts, dps),
        out_shape=(
            jax.ShapeDtypeStruct((tok_rows, quarter), bf),
            jax.ShapeDtypeStruct(logits.shape, jnp.float32),
            jax.ShapeDtypeStruct((quarter, ff), bf),
            jax.ShapeDtypeStruct((quarter, ff), bf),
        ),
        in_specs=[hbm, hbm, vmem, vmem, vmem, hbm, hbm],
        out_specs=(vmem,) * 4,
        scratch_shapes=[
            pltpu.VMEM(w_up.shape, bf),
            pltpu.VMEM(w_down.shape, bf),
            pltpu.VMEM((n, tok_rows, 2 * quarter + 128), bf),
            pltpu.VMEM((n, tok_rows, quarter), bf),
            pltpu.VMEM((n, dps, part_rows, 2 * ff), bf),
            pltpu.VMEM((n, dps, part_rows, 2 * ff), bf),
            pltpu.VMEM((n, part_rows, 2 * ff), bf),
            pltpu.VMEM((n, part_rows, 2 * ff), bf),
            pltpu.VMEM((n, dps, part_rows, ff + 128), bf),
            pltpu.VMEM((n, dps, part_rows, 2 * ff), bf),
            pltpu.VMEM((n, tok_rows, quarter + 128), bf),
            pltpu.VMEM((experts, tok_rows, quarter + 128), bf),
            pltpu.VMEM((experts, tok_rows, quarter + 128), bf),
            pltpu.VMEM((experts, tok_rows, quarter + 128), bf),
            dma((n, 3)), dma((n,)),
            dma((n, dps - 1)), dma((n, dps)),
            dma((n,)), dma((n,)),
            dma((n, dps - 1)), dma((n, dps)),
            dma((n, dps - 1)), dma((n, dps)),
            dma((experts,)), dma((experts,)),
            dma((experts,)), dma((experts,)), dma((4,)),
        ],
        compiler_params=pltpu.CompilerParams(
            collective_id=0, has_side_effects=True, vmem_limit_bytes=56 * 1024 * 1024
        ),
    )(tokens, cotangent, routes, logits, pair_flags.reshape(1, -1), w_up, w_down)


def solution(mesh):
    in_specs = (
        P("expert", "dp"),
        P("expert", None),
        P("expert", None),
        P("expert", "dp"),
        P(),
        P("dp", "expert"),
        P("dp", "expert"),
    )
    small = mesh.shape["expert"] == 8 and mesh.shape["dp"] == 4
    body = one_kernel if small else local
    out_specs = (P("expert", "dp"), P("expert", None), P("dp", "expert"), P("dp", "expert"))
    return jax.shard_map(body, mesh=mesh, in_specs=in_specs, out_specs=out_specs, check_vma=False)
```

```python
import functools
import jax
import jax.numpy as jnp
from jax import lax
from jax.experimental import pallas as pl
from jax.experimental.pallas import tpu as pltpu
from jax.sharding import PartitionSpec as P


def passed_along(value, axis, steps):
    count = lax.axis_size(axis)
    pairs = [(source, (source + steps) % count) for source in range(count)]
    return lax.ppermute(value, axis, pairs)


def pick_pair(swapped_here, theirs, ours):
    return tuple(
        (
            jnp.where(swapped_here, other_part, mine_part)
            for other_part, mine_part in zip(theirs, ours)
        )
    )


def activate(up_pre, grad_hidden):
    up_sig = jax.nn.sigmoid(up_pre)
    hidden = (up_pre * up_sig).astype(jnp.bfloat16)
    pairing_part = jnp.sum(hidden.astype(jnp.float32) * grad_hidden, -1)
    grad_pre = (grad_hidden * up_sig * (1.0 + up_pre * (1.0 - up_sig))).astype(jnp.bfloat16)
    return (hidden, pairing_part, grad_pre)


def local(tokens, routes, logits, cotangent, pair_flags, w_up, w_down):
    devices_ex = lax.axis_size("expert")
    experts = devices_ex // 2
    half_way = experts // 2
    here_index = lax.axis_index("expert")
    slot_here = here_index // 2
    tok_rows, top_count = routes.shape
    quarter = tokens.shape[1]
    capacity = max(2, 2 * (3 * tok_rows * top_count // (4 * experts)))
    expert_ids = jnp.arange(experts, dtype=jnp.int32)
    paired = jnp.concatenate([pair_flags, pair_flags]) > 0
    owner_slot = jnp.where(paired, (expert_ids + half_way) % experts, expert_ids)
    swapped_here = paired[slot_here]
    affinity = jax.nn.sigmoid(logits)
    weights = affinity / jnp.sum(affinity, -1, keepdims=True)
    scaled = (weights[:, :, None] * cotangent[:, None, :].astype(jnp.float32)).astype(jnp.bfloat16)
    scaled = scaled.reshape(-1, quarter)
    flat_routes = routes.reshape(-1)
    onehot = (flat_routes[:, None] == expert_ids[None, :]).astype(jnp.int32)
    route_order = jnp.arange(tok_rows * top_count, dtype=jnp.int32)
    same = flat_routes[:, None] == flat_routes[None, :]
    slot_rank = jnp.sum((same & (route_order[None, :] < route_order[:, None])).astype(jnp.int32), 1)
    own_weights = (w_up, w_down)
    shifted = passed_along((w_up, w_down), "expert", devices_ex // 2)
    resident = pick_pair(swapped_here, shifted, own_weights)
    target = owner_slot[flat_routes]
    position = target * capacity + slot_rank
    empty_rows = jnp.zeros((experts * capacity, quarter), jnp.bfloat16)
    token_buf = (
        empty_rows.at[position]
        .set(jnp.repeat(tokens, top_count, axis=0))
        .reshape(experts, capacity, quarter)
    )
    scaled_buf = empty_rows.at[position].set(scaled).reshape(experts, capacity, quarter)
    token_in, scaled_in = (
        lax.all_to_all(
            jnp.repeat(token_buf, 2, axis=0), "expert", split_axis=0, concat_axis=0, tiled=True
        ),
        lax.all_to_all(
            jnp.repeat(scaled_buf, 2, axis=0), "expert", split_axis=0, concat_axis=0, tiled=True
        ),
    )
    routed_rows = token_in.reshape(-1, quarter)
    scaled_rows = scaled_in.reshape(-1, quarter)
    up_block, down_block = resident
    up_part = jnp.dot(routed_rows, up_block, preferred_element_type=jnp.float32)
    grad_part = jnp.dot(scaled_rows, down_block, preferred_element_type=jnp.float32)
    up_pre, grad_hidden = (
        lax.psum(up_part.astype(jnp.bfloat16), "dp").astype(jnp.float32),
        lax.psum(grad_part.astype(jnp.bfloat16), "dp").astype(jnp.float32),
    )
    hidden, pairing_part, grad_pre = activate(up_pre, grad_hidden)
    pairing_half = pairing_part.astype(jnp.bfloat16)
    route_half = jnp.einsum(
        "nf,df->nd", grad_pre, up_block, preferred_element_type=jnp.float32
    ).astype(jnp.bfloat16)
    grad_up = jnp.einsum(
        "nd,nf->df", routed_rows, grad_pre, preferred_element_type=jnp.float32
    ).astype(jnp.bfloat16)
    grad_down = jnp.einsum(
        "nd,nf->df", scaled_rows, hidden, preferred_element_type=jnp.float32
    ).astype(jnp.bfloat16)
    back_rows, back_pairing = (
        lax.all_to_all(
            route_half.reshape(devices_ex, capacity, quarter),
            "expert",
            split_axis=0,
            concat_axis=0,
            tiled=True,
        ),
        lax.all_to_all(
            pairing_half.reshape(devices_ex, capacity),
            "expert",
            split_axis=0,
            concat_axis=0,
            tiled=True,
        ),
    )
    back_grid = back_rows.reshape(experts, 2, capacity, quarter)
    picked = [
        back_grid[:, half].reshape(-1, quarter)[position].astype(jnp.float32) for half in range(2)
    ]
    grad_tokens = jnp.sum(
        (picked[0] + picked[1]).reshape(tok_rows, top_count, quarter), 1
    ).astype(jnp.bfloat16)
    pair_grid = back_pairing.reshape(experts, 2, capacity)
    pair_picked = pair_grid[target, :, slot_rank]
    pairing_mine = jnp.sum(pair_picked.astype(jnp.float32), 1).reshape(tok_rows, top_count)
    grad_logits = (1.0 - affinity) * (
        pairing_mine - weights * jnp.sum(pairing_mine, -1, keepdims=True)
    )
    return (grad_tokens, grad_logits, grad_up, grad_down)

def everything(
    zs, dps, tok_ref, cot_ref, routes_ref, logits_ref, flags_ref, up_hbm, down_hbm,
    gt_ref, gl_ref, gu_ref, gd_ref,
    up_ref, down_ref,
    rows_all, scaled_slot, part, part_in, mine, theirs, home_g, slot_g, back, back_x, back_z, to_z,
    row_s, row_r, rs_s, rs_r, gh_s, gh_r, home_s, home_r, slot_s, slot_r, bx_s, bx_r, bz_s, bz_r, local_s,
):
    me = lax.axis_index("expert")
    d = lax.axis_index("dp")
    z, x = me // 2, me % 2
    other = z * 2 + 1 - x
    partner = ((z + zs // 2) % zs) * 2 + x
    quarter = tok_ref.shape[1]
    ff = up_ref.shape[1]
    bf, f32 = jnp.bfloat16, jnp.float32

    def remote(src, dst, send, recv, expert, dp):
        return pltpu.make_async_remote_copy(
            src_ref=src, dst_ref=dst, send_sem=send, recv_sem=recv,
            device_id={"expert": expert, "dp": dp}, device_id_type=pl.DeviceIdType.MESH,
        )

    def peer(r):
        return lax.rem(d + r, dps)

    barrier = pltpu.get_barrier_semaphore()
    for r in range(1, zs):
        pl.semaphore_signal(
            barrier, inc=1, device_id={"expert": ((z + r) % zs) * 2 + x, "dp": d},
            device_id_type=pl.DeviceIdType.MESH,
        )
    pl.semaphore_signal(
        barrier, inc=1, device_id={"expert": other, "dp": d}, device_id_type=pl.DeviceIdType.MESH
    )
    for r in range(1, dps):
        pl.semaphore_signal(
            barrier, inc=1, device_id={"expert": me, "dp": peer(r)},
            device_id_type=pl.DeviceIdType.MESH,
        )
    held = [
        pltpu.make_async_copy(tok_ref, rows_all.at[me, :, 0:quarter], local_s.at[0]),
        pltpu.make_async_copy(cot_ref, rows_all.at[me, :, quarter : 2 * quarter], local_s.at[1]),
        pltpu.make_async_copy(up_hbm, up_ref, local_s.at[2]),
        pltpu.make_async_copy(down_hbm, down_ref, local_s.at[3]),
    ]
    for copy in held:
        copy.start()
    affinity = jax.nn.sigmoid(logits_ref[...])
    weights = affinity / jnp.sum(affinity, -1, keepdims=True)
    lanes = lax.broadcasted_iota(jnp.int32, (tok_ref.shape[0], 128), 1)
    group = jnp.where(lanes < 96, lanes % 32, 32)
    tops = logits_ref.shape[1]
    whole = jnp.zeros(lanes.shape, f32)
    for k in range(tops):
        whole = whole + jnp.where(routes_ref[:, k : k + 1] == group, weights[:, k : k + 1], 0.0)
    pair_lane = lax.broadcasted_iota(jnp.int32, flags_ref.shape, 1)
    swap = jnp.sum(
        jnp.where((pair_lane == z % (zs // 2)) & (flags_ref[...] > 0), 1.0, 0.0), 1, keepdims=True
    )
    group_row = group[0:1, :]
    pick_home = jnp.where(group_row == z, 1.0, 0.0)
    pick_far = jnp.where(group_row == (z + zs // 2) % zs, 1.0, 0.0)
    pick_slot = pick_home * (1.0 - swap) + pick_far * swap
    high = whole.astype(bf).astype(f32)
    middle = (whole - high).astype(bf).astype(f32)
    low = whole - high - middle
    terms = jnp.where(lanes < 32, high, jnp.where(lanes < 64, middle, low))
    rows_all[me, :, 2 * quarter :] = terms.astype(bf)
    for copy in held:
        copy.wait()
    pl.semaphore_wait(barrier, zs - 1 + 1 + dps - 1)

    def row_copy(b, way, expert):
        return remote(
            rows_all.at[b], rows_all.at[b], row_s.at[b, way], row_r.at[b], expert, d
        )

    def rs_copy(b, r):
        return remote(
            part.at[b, peer(r)], part_in.at[b, d], rs_s.at[b, r - 1], rs_r.at[b, d], me, peer(r)
        )

    def gh_copy(b):
        return remote(mine.at[b], theirs.at[b], gh_s.at[b], gh_r.at[b], partner, d)

    def home_copy(b, r):
        return remote(
            home_g.at[b, d], home_g.at[b, d], home_s.at[b, r - 1], home_r.at[b, d], me, peer(r)
        )

    core = d + 1 - 2 * (d % 2)
    across = (d + 2) % 4
    corner = (core + 2) % 4

    def slot_copy(b, way):
        piece = across if way == 2 else d
        target = across if way == 1 else core
        return remote(
            slot_g.at[b, piece], slot_g.at[b, piece], slot_s.at[b, way], slot_r.at[b, piece],
            me, target,
        )

    def slot_wait(b, piece, source):
        remote(
            slot_g.at[b, d], slot_g.at[b, piece], slot_s.at[b, 0], slot_r.at[b, piece], me, source
        ).wait_recv()

    def zz_of(j):
        far = (j + 1) // 2
        return jnp.where(j % 2 == 1, z + far, z - far)

    def valid(j):
        zz = zz_of(j)
        return (j >= 0) & (j < 2 * zs - 1) & (zz >= 0) & (zz < zs)

    def multiply(b):
        ext = rows_all[b, :, 2 * quarter :].astype(f32)
        cot = rows_all[b, :, quarter : 2 * quarter].astype(f32)
        w_home = jnp.sum(ext * pick_home, axis=1, keepdims=True)
        w_slot = jnp.sum(ext * pick_slot, axis=1, keepdims=True)
        up = jnp.dot(rows_all[b, :, 0:quarter], up_ref[...], preferred_element_type=f32)
        part[b, :, :, 0:ff] = up.astype(bf).reshape(dps, -1, ff)
        scaled = (w_home * cot).astype(bf)
        grad = jnp.dot(scaled, down_ref[...], preferred_element_type=f32)
        part[b, :, :, ff:] = grad.astype(bf).reshape(dps, -1, ff)
        for r in range(1, dps):
            rs_copy(b, r).start()
        scaled_slot[b] = (w_slot * cot).astype(bf)

    def act(b):
        for r in range(1, dps):
            remote(
                part.at[b, peer(r)], part_in.at[b, peer(r)], rs_s.at[b, r - 1],
                rs_r.at[b, peer(r)], me, peer(r),
            ).wait_recv()
        total = part[b, d].astype(f32)
        for r in range(1, dps):
            total = total + part_in[b, peer(r)].astype(f32)
        hidden, pairing, grad_pre = activate(total[:, 0:ff], total[:, ff:])
        mine[b, :, 0:ff] = grad_pre
        mine[b, :, ff:] = hidden
        gh_copy(b).start()
        at = lax.broadcasted_iota(jnp.int32, (grad_pre.shape[0], 128), 1)
        home_g[b, d, :, 0:ff] = grad_pre
        home_g[b, d, :, ff:] = jnp.where(at == z, pairing[:, None], 0.0).astype(bf)
        for r in range(1, dps):
            home_copy(b, r).start()

    def back_rows(b):
        for r in range(1, dps):
            remote(
                home_g.at[b, d], home_g.at[b, peer(r)], home_s.at[b, r - 1],
                home_r.at[b, peer(r)], me, peer(r),
            ).wait_recv()
        joined = home_g[b].reshape(-1, ff + 128)
        rows = lax.dot_general(
            joined[:, 0:ff], up_ref[...], (((1,), (1,)), ((), ())), preferred_element_type=f32
        )
        back[b, :, 0:quarter] = rows.astype(bf)
        back[b, :, quarter:] = joined[:, ff:]

    def bx_copy(zz):
        return remote(
            back.at[zz * 2 + 1 - x], back_x.at[zz], bx_s.at[zz], bx_r.at[zz], other, d
        )

    def bz_copy(zz):
        return remote(to_z.at[zz], back_z.at[z], bz_s.at[zz], bz_r.at[z], zz * 2 + x, d)

    def first(j, _):
        zz = zz_of(j)

        @pl.when(valid(j))
        def _():
            b = zz * 2 + x

            @pl.when(j > 0)
            def _():
                row_copy(b, 0, me).wait_recv()

            @pl.when((zz <= z) & (z < zs - 1))
            def _():
                row_copy(b, 0, me + 2).start()

            @pl.when((zz >= z) & (z > 0))
            def _():
                row_copy(b, 1, me - 2).start()

            row_copy(b, 2, other).start()
            multiply(b)

        @pl.when(valid(j - 1))
        def _():
            b = zz_of(j - 1) * 2 + 1 - x
            row_copy(b, 2, other).wait_recv()
            multiply(b)
            act(zz_of(j - 1) * 2 + x)

        @pl.when(valid(j - 2))
        def _():
            act(zz_of(j - 2) * 2 + 1 - x)
            back_rows(zz_of(j - 2) * 2 + x)

        @pl.when(valid(j - 3))
        def _():
            back_rows(zz_of(j - 3) * 2 + 1 - x)
            bx_copy(zz_of(j - 3)).start()

        return 0

    lax.fori_loop(0, 2 * zs + 2, first, 0)

    def slot_forward(b):
        slot_wait(b, across, across)
        slot_copy(b, 2).start()

    def second(j, _):
        @pl.when(valid(j))
        def _():
            for side in range(2):
                b = ((zz_of(j) + zs // 2) % zs) * 2 + side
                gh_copy(b).wait_recv()
                picked = mine[b].astype(f32) * (1.0 - swap) + theirs[b].astype(f32) * swap
                slot_g[b, d] = picked.astype(bf)
                slot_copy(b, 1).start()
                slot_copy(b, 0).start()

        @pl.when(valid(j - 1))
        def _():
            for side in range(2):
                slot_forward(((zz_of(j - 1) + zs // 2) % zs) * 2 + side)

        return 0

    lax.fori_loop(0, 2 * zs, second, 0)

    def fourth(j, _):
        zz = zz_of(j)
        b = zz * 2 + x

        @pl.when(valid(j))
        def _():
            bx_copy(zz).wait_recv()

        @pl.when(valid(j) & (zz != z))
        def _():
            to_z[zz] = (back[b].astype(f32) + back_x[zz].astype(f32)).astype(bf)
            bz_copy(zz).start()

        @pl.when(valid(j) & (zz == z))
        def _():
            back_z[z] = (back[b].astype(f32) + back_x[zz].astype(f32)).astype(bf)

        return 0

    lax.fori_loop(0, 2 * zs - 1, fourth, 0)

    def slot_rest(b, _):
        slot_wait(b, core, core)
        slot_wait(b, corner, core)
        return 0

    lax.fori_loop(0, 2 * zs, slot_rest, 0)

    for low_at in range(0, quarter, 512):
        at = slice(low_at, min(low_at + 512, quarter))
        tokens = rows_all[:, :, at].reshape(-1, at.stop - at.start)
        gu_ref[at, :] = lax.dot_general(
            tokens, slot_g[:, :, :, 0:ff].reshape(-1, ff), (((0,), (0,)), ((), ())),
            preferred_element_type=f32,
        ).astype(bf)
        scaled = scaled_slot[:, :, at].reshape(-1, at.stop - at.start)
        gd_ref[at, :] = lax.dot_general(
            scaled, slot_g[:, :, :, ff:].reshape(-1, ff), (((0,), (0,)), ((), ())),
            preferred_element_type=f32,
        ).astype(bf)

    for r in range(1, zs):
        zz = (z + r) % zs
        remote(to_z.at[zz], back_z.at[zz], bz_s.at[zz], bz_r.at[zz], zz * 2 + x, d).wait_recv()
    total = back_z[0].astype(f32)
    for r in range(1, zs):
        total = total + back_z[r].astype(f32)
    gt_ref[...] = total[:, 0:quarter].astype(bf)
    pairs = total[:, quarter:]
    pairing = [
        jnp.sum(jnp.where(lanes == routes_ref[:, k : k + 1], pairs, 0.0), 1, keepdims=True)
        for k in range(tops)
    ]
    across_k = sum(pairing[1:], pairing[0])
    for k in range(tops):
        gl_ref[:, k : k + 1] = (1.0 - affinity[:, k : k + 1]) * (
            pairing[k] - weights[:, k : k + 1] * across_k
        )

    def drain(b, _):
        zz = b // 2

        @pl.when(b % 2 == x)
        def _():
            @pl.when((zz <= z) & (z < zs - 1))
            def _():
                row_copy(b, 0, me + 2).wait_send()

            @pl.when((zz >= z) & (z > 0))
            def _():
                row_copy(b, 1, me - 2).wait_send()

            row_copy(b, 2, other).wait_send()

            @pl.when(zz != z)
            def _():
                bz_copy(zz).wait_send()

            bx_copy(zz).wait_send()

        for r in range(1, dps):
            rs_copy(b, r).wait_send()
            home_copy(b, r).wait_send()
            slot_copy(b, r - 1).wait_send()
        gh_copy(b).wait_send()
        return 0

    lax.fori_loop(0, 2 * zs, drain, 0)


def one_kernel(tokens, routes, logits, cotangent, pair_flags, w_up, w_down):
    devices_ex = lax.axis_size("expert")
    dps = lax.axis_size("dp")
    experts = devices_ex // 2
    tok_rows = routes.shape[0]
    quarter = tokens.shape[1]
    ff = w_up.shape[1]
    bf = jnp.bfloat16
    part_rows = tok_rows // dps
    vmem = pl.BlockSpec(memory_space=pltpu.VMEM)
    hbm = pl.BlockSpec(memory_space=pl.ANY)
    dma = pltpu.SemaphoreType.DMA
    n = devices_ex
    return pl.pallas_call(
        functools.partial(everything, experts, dps),
        out_shape=(
            jax.ShapeDtypeStruct((tok_rows, quarter), bf),
            jax.ShapeDtypeStruct(logits.shape, jnp.float32),
            jax.ShapeDtypeStruct((quarter, ff), bf),
            jax.ShapeDtypeStruct((quarter, ff), bf),
        ),
        in_specs=[hbm, hbm, vmem, vmem, vmem, hbm, hbm],
        out_specs=(vmem,) * 4,
        scratch_shapes=[
            pltpu.VMEM(w_up.shape, bf),
            pltpu.VMEM(w_down.shape, bf),
            pltpu.VMEM((n, tok_rows, 2 * quarter + 128), bf),
            pltpu.VMEM((n, tok_rows, quarter), bf),
            pltpu.VMEM((n, dps, part_rows, 2 * ff), bf),
            pltpu.VMEM((n, dps, part_rows, 2 * ff), bf),
            pltpu.VMEM((n, part_rows, 2 * ff), bf),
            pltpu.VMEM((n, part_rows, 2 * ff), bf),
            pltpu.VMEM((n, dps, part_rows, ff + 128), bf),
            pltpu.VMEM((n, dps, part_rows, 2 * ff), bf),
            pltpu.VMEM((n, tok_rows, quarter + 128), bf),
            pltpu.VMEM((experts, tok_rows, quarter + 128), bf),
            pltpu.VMEM((experts, tok_rows, quarter + 128), bf),
            pltpu.VMEM((experts, tok_rows, quarter + 128), bf),
            dma((n, 3)), dma((n,)),
            dma((n, dps - 1)), dma((n, dps)),
            dma((n,)), dma((n,)),
            dma((n, dps - 1)), dma((n, dps)),
            dma((n, dps - 1)), dma((n, dps)),
            dma((experts,)), dma((experts,)),
            dma((experts,)), dma((experts,)), dma((4,)),
        ],
        compiler_params=pltpu.CompilerParams(
            collective_id=0, has_side_effects=True, vmem_limit_bytes=56 * 1024 * 1024
        ),
    )(tokens, cotangent, routes, logits, pair_flags.reshape(1, -1), w_up, w_down)


def solution(mesh):
    in_specs = (
        P("expert", "dp"),
        P("expert", None),
        P("expert", None),
        P("expert", "dp"),
        P(),
        P("dp", "expert"),
        P("dp", "expert"),
    )
    small = mesh.shape["expert"] == 8 and mesh.shape["dp"] == 4
    body = one_kernel if small else local
    out_specs = (P("expert", "dp"), P("expert", None), P("dp", "expert"), P("dp", "expert"))
    return jax.shard_map(body, mesh=mesh, in_specs=in_specs, out_specs=out_specs, check_vma=False)
```

```python
import functools
import jax
import jax.numpy as jnp
from jax import lax
from jax.experimental import pallas as pl
from jax.experimental.pallas import tpu as pltpu
from jax.sharding import PartitionSpec as P


def passed_along(value, axis, steps):
    count = lax.axis_size(axis)
    pairs = [(source, (source + steps) % count) for source in range(count)]
    return lax.ppermute(value, axis, pairs)


def pick_pair(swapped_here, theirs, ours):
    return tuple(
        (
            jnp.where(swapped_here, other_part, mine_part)
            for other_part, mine_part in zip(theirs, ours)
        )
    )


def activate(up_pre, grad_hidden):
    up_sig = jax.nn.sigmoid(up_pre)
    hidden = (up_pre * up_sig).astype(jnp.bfloat16)
    pairing_part = jnp.sum(hidden.astype(jnp.float32) * grad_hidden, -1)
    grad_pre = (grad_hidden * up_sig * (1.0 + up_pre * (1.0 - up_sig))).astype(jnp.bfloat16)
    return (hidden, pairing_part, grad_pre)


def local(tokens, routes, logits, cotangent, pair_flags, w_up, w_down):
    devices_ex = lax.axis_size("expert")
    experts = devices_ex // 2
    half_way = experts // 2
    here_index = lax.axis_index("expert")
    slot_here = here_index // 2
    tok_rows, top_count = routes.shape
    quarter = tokens.shape[1]
    capacity = max(2, 2 * (3 * tok_rows * top_count // (4 * experts)))
    expert_ids = jnp.arange(experts, dtype=jnp.int32)
    paired = jnp.concatenate([pair_flags, pair_flags]) > 0
    owner_slot = jnp.where(paired, (expert_ids + half_way) % experts, expert_ids)
    swapped_here = paired[slot_here]
    affinity = jax.nn.sigmoid(logits)
    weights = affinity / jnp.sum(affinity, -1, keepdims=True)
    scaled = (weights[:, :, None] * cotangent[:, None, :].astype(jnp.float32)).astype(jnp.bfloat16)
    scaled = scaled.reshape(-1, quarter)
    flat_routes = routes.reshape(-1)
    onehot = (flat_routes[:, None] == expert_ids[None, :]).astype(jnp.int32)
    route_order = jnp.arange(tok_rows * top_count, dtype=jnp.int32)
    same = flat_routes[:, None] == flat_routes[None, :]
    slot_rank = jnp.sum((same & (route_order[None, :] < route_order[:, None])).astype(jnp.int32), 1)
    own_weights = (w_up, w_down)
    shifted = passed_along((w_up, w_down), "expert", devices_ex // 2)
    resident = pick_pair(swapped_here, shifted, own_weights)
    target = owner_slot[flat_routes]
    position = target * capacity + slot_rank
    empty_rows = jnp.zeros((experts * capacity, quarter), jnp.bfloat16)
    token_buf = (
        empty_rows.at[position]
        .set(jnp.repeat(tokens, top_count, axis=0))
        .reshape(experts, capacity, quarter)
    )
    scaled_buf = empty_rows.at[position].set(scaled).reshape(experts, capacity, quarter)
    token_in, scaled_in = (
        lax.all_to_all(
            jnp.repeat(token_buf, 2, axis=0), "expert", split_axis=0, concat_axis=0, tiled=True
        ),
        lax.all_to_all(
            jnp.repeat(scaled_buf, 2, axis=0), "expert", split_axis=0, concat_axis=0, tiled=True
        ),
    )
    routed_rows = token_in.reshape(-1, quarter)
    scaled_rows = scaled_in.reshape(-1, quarter)
    up_block, down_block = resident
    up_part = jnp.dot(routed_rows, up_block, preferred_element_type=jnp.float32)
    grad_part = jnp.dot(scaled_rows, down_block, preferred_element_type=jnp.float32)
    up_pre, grad_hidden = (
        lax.psum(up_part.astype(jnp.bfloat16), "dp").astype(jnp.float32),
        lax.psum(grad_part.astype(jnp.bfloat16), "dp").astype(jnp.float32),
    )
    hidden, pairing_part, grad_pre = activate(up_pre, grad_hidden)
    pairing_half = pairing_part.astype(jnp.bfloat16)
    route_half = jnp.einsum(
        "nf,df->nd", grad_pre, up_block, preferred_element_type=jnp.float32
    ).astype(jnp.bfloat16)
    grad_up = jnp.einsum(
        "nd,nf->df", routed_rows, grad_pre, preferred_element_type=jnp.float32
    ).astype(jnp.bfloat16)
    grad_down = jnp.einsum(
        "nd,nf->df", scaled_rows, hidden, preferred_element_type=jnp.float32
    ).astype(jnp.bfloat16)
    back_rows, back_pairing = (
        lax.all_to_all(
            route_half.reshape(devices_ex, capacity, quarter),
            "expert",
            split_axis=0,
            concat_axis=0,
            tiled=True,
        ),
        lax.all_to_all(
            pairing_half.reshape(devices_ex, capacity),
            "expert",
            split_axis=0,
            concat_axis=0,
            tiled=True,
        ),
    )
    back_grid = back_rows.reshape(experts, 2, capacity, quarter)
    picked = [
        back_grid[:, half].reshape(-1, quarter)[position].astype(jnp.float32) for half in range(2)
    ]
    grad_tokens = jnp.sum(
        (picked[0] + picked[1]).reshape(tok_rows, top_count, quarter), 1
    ).astype(jnp.bfloat16)
    pair_grid = back_pairing.reshape(experts, 2, capacity)
    pair_picked = pair_grid[target, :, slot_rank]
    pairing_mine = jnp.sum(pair_picked.astype(jnp.float32), 1).reshape(tok_rows, top_count)
    grad_logits = (1.0 - affinity) * (
        pairing_mine - weights * jnp.sum(pairing_mine, -1, keepdims=True)
    )
    return (grad_tokens, grad_logits, grad_up, grad_down)

def everything(
    zs, dps, tok_ref, cot_ref, routes_ref, logits_ref, flags_ref, up_hbm, down_hbm,
    gt_ref, gl_ref, gu_ref, gd_ref,
    up_ref, down_ref,
    rows_all, scaled_slot, part, part_in, mine, theirs, home_g, slot_g, back, back_x, back_z, to_z,
    row_s, row_r, rs_s, rs_r, gh_s, gh_r, home_s, home_r, slot_s, slot_r, bx_s, bx_r, bz_s, bz_r, local_s,
):
    me = lax.axis_index("expert")
    d = lax.axis_index("dp")
    z, x = me // 2, me % 2
    other = z * 2 + 1 - x
    partner = ((z + zs // 2) % zs) * 2 + x
    quarter = tok_ref.shape[1]
    ff = up_ref.shape[1]
    bf, f32 = jnp.bfloat16, jnp.float32

    def remote(src, dst, send, recv, expert, dp):
        return pltpu.make_async_remote_copy(
            src_ref=src, dst_ref=dst, send_sem=send, recv_sem=recv,
            device_id={"expert": expert, "dp": dp}, device_id_type=pl.DeviceIdType.MESH,
        )

    def peer(r):
        return lax.rem(d + r, dps)

    barrier = pltpu.get_barrier_semaphore()
    for r in range(1, zs):
        pl.semaphore_signal(
            barrier, inc=1, device_id={"expert": ((z + r) % zs) * 2 + x, "dp": d},
            device_id_type=pl.DeviceIdType.MESH,
        )
    pl.semaphore_signal(
        barrier, inc=1, device_id={"expert": other, "dp": d}, device_id_type=pl.DeviceIdType.MESH
    )
    for r in range(1, dps):
        pl.semaphore_signal(
            barrier, inc=1, device_id={"expert": me, "dp": peer(r)},
            device_id_type=pl.DeviceIdType.MESH,
        )
    held = [
        pltpu.make_async_copy(tok_ref, rows_all.at[me, :, 0:quarter], local_s.at[0]),
        pltpu.make_async_copy(cot_ref, rows_all.at[me, :, quarter : 2 * quarter], local_s.at[1]),
        pltpu.make_async_copy(up_hbm, up_ref, local_s.at[2]),
        pltpu.make_async_copy(down_hbm, down_ref, local_s.at[3]),
    ]
    for copy in held:
        copy.start()
    affinity = jax.nn.sigmoid(logits_ref[...])
    weights = affinity / jnp.sum(affinity, -1, keepdims=True)
    lanes = lax.broadcasted_iota(jnp.int32, (tok_ref.shape[0], 128), 1)
    group = jnp.where(lanes < 96, lanes % 32, 32)
    tops = logits_ref.shape[1]
    whole = jnp.zeros(lanes.shape, f32)
    for k in range(tops):
        whole = whole + jnp.where(routes_ref[:, k : k + 1] == group, weights[:, k : k + 1], 0.0)
    pair_lane = lax.broadcasted_iota(jnp.int32, flags_ref.shape, 1)
    swap = jnp.sum(
        jnp.where((pair_lane == z % (zs // 2)) & (flags_ref[...] > 0), 1.0, 0.0), 1, keepdims=True
    )
    group_row = group[0:1, :]
    pick_home = jnp.where(group_row == z, 1.0, 0.0)
    pick_far = jnp.where(group_row == (z + zs // 2) % zs, 1.0, 0.0)
    pick_slot = pick_home * (1.0 - swap) + pick_far * swap
    high = whole.astype(bf).astype(f32)
    middle = (whole - high).astype(bf).astype(f32)
    low = whole - high - middle
    terms = jnp.where(lanes < 32, high, jnp.where(lanes < 64, middle, low))
    rows_all[me, :, 2 * quarter :] = terms.astype(bf)
    for copy in held:
        copy.wait()
    pl.semaphore_wait(barrier, zs - 1 + 1 + dps - 1)

    def row_copy(b, way, expert):
        return remote(
            rows_all.at[b], rows_all.at[b], row_s.at[b, way], row_r.at[b], expert, d
        )

    def rs_copy(b, r):
        return remote(
            part.at[b, peer(r)], part_in.at[b, d], rs_s.at[b, r - 1], rs_r.at[b, d], me, peer(r)
        )

    def gh_copy(b):
        return remote(mine.at[b], theirs.at[b], gh_s.at[b], gh_r.at[b], partner, d)

    def home_copy(b, r):
        return remote(
            home_g.at[b, d], home_g.at[b, d], home_s.at[b, r - 1], home_r.at[b, d], me, peer(r)
        )

    core = d + 1 - 2 * (d % 2)
    across = (d + 2) % 4
    corner = (core + 2) % 4

    def slot_copy(b, way):
        piece = across if way == 2 else d
        target = across if way == 1 else core
        return remote(
            slot_g.at[b, piece], slot_g.at[b, piece], slot_s.at[b, way], slot_r.at[b, piece],
            me, target,
        )

    def slot_wait(b, piece, source):
        remote(
            slot_g.at[b, d], slot_g.at[b, piece], slot_s.at[b, 0], slot_r.at[b, piece], me, source
        ).wait_recv()

    def zz_of(j):
        far = (j + 1) // 2
        return jnp.where(j % 2 == 1, z + far, z - far)

    def valid(j):
        zz = zz_of(j)
        return (j >= 0) & (j < 2 * zs - 1) & (zz >= 0) & (zz < zs)

    def multiply(b):
        ext = rows_all[b, :, 2 * quarter :].astype(f32)
        cot = rows_all[b, :, quarter : 2 * quarter].astype(f32)
        w_home = jnp.sum(ext * pick_home, axis=1, keepdims=True)
        w_slot = jnp.sum(ext * pick_slot, axis=1, keepdims=True)
        up = jnp.dot(rows_all[b, :, 0:quarter], up_ref[...], preferred_element_type=f32)
        part[b, :, :, 0:ff] = up.astype(bf).reshape(dps, -1, ff)
        scaled = (w_home * cot).astype(bf)
        grad = jnp.dot(scaled, down_ref[...], preferred_element_type=f32)
        part[b, :, :, ff:] = grad.astype(bf).reshape(dps, -1, ff)
        for r in range(1, dps):
            rs_copy(b, r).start()
        scaled_slot[b] = (w_slot * cot).astype(bf)

    def act(b):
        for r in range(1, dps):
            remote(
                part.at[b, peer(r)], part_in.at[b, peer(r)], rs_s.at[b, r - 1],
                rs_r.at[b, peer(r)], me, peer(r),
            ).wait_recv()
        total = part[b, d].astype(f32)
        for r in range(1, dps):
            total = total + part_in[b, peer(r)].astype(f32)
        hidden, pairing, grad_pre = activate(total[:, 0:ff], total[:, ff:])
        mine[b, :, 0:ff] = grad_pre
        mine[b, :, ff:] = hidden
        gh_copy(b).start()
        at = lax.broadcasted_iota(jnp.int32, (grad_pre.shape[0], 128), 1)
        home_g[b, d, :, 0:ff] = grad_pre
        home_g[b, d, :, ff:] = jnp.where(at == z, pairing[:, None], 0.0).astype(bf)
        for r in range(1, dps):
            home_copy(b, r).start()

    def back_rows(b):
        for r in range(1, dps):
            remote(
                home_g.at[b, d], home_g.at[b, peer(r)], home_s.at[b, r - 1],
                home_r.at[b, peer(r)], me, peer(r),
            ).wait_recv()
        joined = home_g[b].reshape(-1, ff + 128)
        rows = lax.dot_general(
            joined[:, 0:ff], up_ref[...], (((1,), (1,)), ((), ())), preferred_element_type=f32
        )
        back[b, :, 0:quarter] = rows.astype(bf)
        back[b, :, quarter:] = joined[:, ff:]

    def bx_copy(zz):
        return remote(
            back.at[zz * 2 + 1 - x], back_x.at[zz], bx_s.at[zz], bx_r.at[zz], other, d
        )

    def bz_copy(zz):
        return remote(to_z.at[zz], back_z.at[z], bz_s.at[zz], bz_r.at[z], zz * 2 + x, d)

    def first(j, _):
        zz = zz_of(j)

        @pl.when(valid(j))
        def _():
            b = zz * 2 + x

            @pl.when(j > 0)
            def _():
                row_copy(b, 0, me).wait_recv()

            @pl.when((zz <= z) & (z < zs - 1))
            def _():
                row_copy(b, 0, me + 2).start()

            @pl.when((zz >= z) & (z > 0))
            def _():
                row_copy(b, 1, me - 2).start()

            row_copy(b, 2, other).start()
            multiply(b)

        @pl.when(valid(j - 1))
        def _():
            b = zz_of(j - 1) * 2 + 1 - x
            row_copy(b, 2, other).wait_recv()
            multiply(b)
            act(zz_of(j - 1) * 2 + x)

        @pl.when(valid(j - 2))
        def _():
            act(zz_of(j - 2) * 2 + 1 - x)
            back_rows(zz_of(j - 2) * 2 + x)

        @pl.when(valid(j - 3))
        def _():
            back_rows(zz_of(j - 3) * 2 + 1 - x)

        return 0

    lax.fori_loop(0, 2 * zs + 2, first, 0)

    def start_back(zz, _):
        bx_copy(zz).start()
        return 0

    lax.fori_loop(0, zs, start_back, 0)

    def slot_forward(b):
        slot_wait(b, across, across)
        slot_copy(b, 2).start()

    def second(j, _):
        @pl.when(valid(j))
        def _():
            for side in range(2):
                b = ((zz_of(j) + zs // 2) % zs) * 2 + side
                gh_copy(b).wait_recv()
                picked = mine[b].astype(f32) * (1.0 - swap) + theirs[b].astype(f32) * swap
                slot_g[b, d] = picked.astype(bf)
                slot_copy(b, 1).start()
                slot_copy(b, 0).start()

        @pl.when(valid(j - 1))
        def _():
            for side in range(2):
                slot_forward(((zz_of(j - 1) + zs // 2) % zs) * 2 + side)

        return 0

    lax.fori_loop(0, 2 * zs, second, 0)

    def fourth(j, _):
        zz = zz_of(j)
        b = zz * 2 + x

        @pl.when(valid(j))
        def _():
            bx_copy(zz).wait_recv()

        @pl.when(valid(j) & (zz != z))
        def _():
            to_z[zz] = (back[b].astype(f32) + back_x[zz].astype(f32)).astype(bf)
            bz_copy(zz).start()

        @pl.when(valid(j) & (zz == z))
        def _():
            back_z[z] = (back[b].astype(f32) + back_x[zz].astype(f32)).astype(bf)

        return 0

    lax.fori_loop(0, 2 * zs - 1, fourth, 0)

    def slot_rest(b, _):
        slot_wait(b, core, core)
        slot_wait(b, corner, core)
        return 0

    lax.fori_loop(0, 2 * zs, slot_rest, 0)

    for low_at in range(0, quarter, 512):
        at = slice(low_at, min(low_at + 512, quarter))
        tokens = rows_all[:, :, at].reshape(-1, at.stop - at.start)
        gu_ref[at, :] = lax.dot_general(
            tokens, slot_g[:, :, :, 0:ff].reshape(-1, ff), (((0,), (0,)), ((), ())),
            preferred_element_type=f32,
        ).astype(bf)
        scaled = scaled_slot[:, :, at].reshape(-1, at.stop - at.start)
        gd_ref[at, :] = lax.dot_general(
            scaled, slot_g[:, :, :, ff:].reshape(-1, ff), (((0,), (0,)), ((), ())),
            preferred_element_type=f32,
        ).astype(bf)

    for r in range(1, zs):
        zz = (z + r) % zs
        remote(to_z.at[zz], back_z.at[zz], bz_s.at[zz], bz_r.at[zz], zz * 2 + x, d).wait_recv()
    total = back_z[0].astype(f32)
    for r in range(1, zs):
        total = total + back_z[r].astype(f32)
    gt_ref[...] = total[:, 0:quarter].astype(bf)
    pairs = total[:, quarter:]
    pairing = [
        jnp.sum(jnp.where(lanes == routes_ref[:, k : k + 1], pairs, 0.0), 1, keepdims=True)
        for k in range(tops)
    ]
    across_k = sum(pairing[1:], pairing[0])
    for k in range(tops):
        gl_ref[:, k : k + 1] = (1.0 - affinity[:, k : k + 1]) * (
            pairing[k] - weights[:, k : k + 1] * across_k
        )

    def drain(b, _):
        zz = b // 2

        @pl.when(b % 2 == x)
        def _():
            @pl.when((zz <= z) & (z < zs - 1))
            def _():
                row_copy(b, 0, me + 2).wait_send()

            @pl.when((zz >= z) & (z > 0))
            def _():
                row_copy(b, 1, me - 2).wait_send()

            row_copy(b, 2, other).wait_send()

            @pl.when(zz != z)
            def _():
                bz_copy(zz).wait_send()

            bx_copy(zz).wait_send()

        for r in range(1, dps):
            rs_copy(b, r).wait_send()
            home_copy(b, r).wait_send()
            slot_copy(b, r - 1).wait_send()
        gh_copy(b).wait_send()
        return 0

    lax.fori_loop(0, 2 * zs, drain, 0)


def one_kernel(tokens, routes, logits, cotangent, pair_flags, w_up, w_down):
    devices_ex = lax.axis_size("expert")
    dps = lax.axis_size("dp")
    experts = devices_ex // 2
    tok_rows = routes.shape[0]
    quarter = tokens.shape[1]
    ff = w_up.shape[1]
    bf = jnp.bfloat16
    part_rows = tok_rows // dps
    vmem = pl.BlockSpec(memory_space=pltpu.VMEM)
    hbm = pl.BlockSpec(memory_space=pl.ANY)
    dma = pltpu.SemaphoreType.DMA
    n = devices_ex
    return pl.pallas_call(
        functools.partial(everything, experts, dps),
        out_shape=(
            jax.ShapeDtypeStruct((tok_rows, quarter), bf),
            jax.ShapeDtypeStruct(logits.shape, jnp.float32),
            jax.ShapeDtypeStruct((quarter, ff), bf),
            jax.ShapeDtypeStruct((quarter, ff), bf),
        ),
        in_specs=[hbm, hbm, vmem, vmem, vmem, hbm, hbm],
        out_specs=(vmem,) * 4,
        scratch_shapes=[
            pltpu.VMEM(w_up.shape, bf),
            pltpu.VMEM(w_down.shape, bf),
            pltpu.VMEM((n, tok_rows, 2 * quarter + 128), bf),
            pltpu.VMEM((n, tok_rows, quarter), bf),
            pltpu.VMEM((n, dps, part_rows, 2 * ff), bf),
            pltpu.VMEM((n, dps, part_rows, 2 * ff), bf),
            pltpu.VMEM((n, part_rows, 2 * ff), bf),
            pltpu.VMEM((n, part_rows, 2 * ff), bf),
            pltpu.VMEM((n, dps, part_rows, ff + 128), bf),
            pltpu.VMEM((n, dps, part_rows, 2 * ff), bf),
            pltpu.VMEM((n, tok_rows, quarter + 128), bf),
            pltpu.VMEM((experts, tok_rows, quarter + 128), bf),
            pltpu.VMEM((experts, tok_rows, quarter + 128), bf),
            pltpu.VMEM((experts, tok_rows, quarter + 128), bf),
            dma((n, 3)), dma((n,)),
            dma((n, dps - 1)), dma((n, dps)),
            dma((n,)), dma((n,)),
            dma((n, dps - 1)), dma((n, dps)),
            dma((n, dps - 1)), dma((n, dps)),
            dma((experts,)), dma((experts,)),
            dma((experts,)), dma((experts,)), dma((4,)),
        ],
        compiler_params=pltpu.CompilerParams(
            collective_id=0, has_side_effects=True, vmem_limit_bytes=56 * 1024 * 1024
        ),
    )(tokens, cotangent, routes, logits, pair_flags.reshape(1, -1), w_up, w_down)


def solution(mesh):
    in_specs = (
        P("expert", "dp"),
        P("expert", None),
        P("expert", None),
        P("expert", "dp"),
        P(),
        P("dp", "expert"),
        P("dp", "expert"),
    )
    small = mesh.shape["expert"] == 8 and mesh.shape["dp"] == 4
    body = one_kernel if small else local
    out_specs = (P("expert", "dp"), P("expert", None), P("dp", "expert"), P("dp", "expert"))
    return jax.shard_map(body, mesh=mesh, in_specs=in_specs, out_specs=out_specs, check_vma=False)
```
